256 devices in a mesh: azi: 64 (over x, y_hi, z), axial: 4 (over y_lo, core).
Axes of the slice: x: 4, y: 4 (y_hi: 2, y_lo: 2; y = y_hi * 2 + y_lo), z: 8, core: 2. Of those that a mesh axis runs over, the one named last changes fastest.
Arguments:
- source_terms: float32 [3, 32, 64, 8192], P(None, 'axial', None, 'azi'), may hold values from -6 to 6
- diffusion: float32 [3, 32, 64, 8192], P(None, 'axial', None, 'azi'), may hold values from 0.5 to 5
- mass_coefficient: float32 [32, 64, 8192], P('axial', None, 'azi'), may hold values from 5 to 50
Outputs:
- solution: float32 [3, 32, 64, 8192], P(None, 'axial', None, 'azi')
- residual: float32 [3, 32, 64, 8192], P(None, 'axial', None, 'azi')
The draws below stay inside these ranges and needn't reach their ends.
All inputs are finite; a program needn't handle non-finite values.
Results may differ from the reference program's by a relative error of at most 0.015.
Values sent between devices are 32-bit elements; how exact they have to be, the bound alone decides.
A program may use at most 64 MiB of HBM per device.

```python
import math
import jax
import jax.numpy as jnp
import numpy as np
from jax import lax

FIELDS = 3
ITERS = 2
NA = 8192
NZ = 32
NR = 64


def steps_of(own_key, shape, cuts, smallest, largest):
    level = 1.0
    for dim, shards_of in cuts:
        steps = jax.random.uniform(jax.random.fold_in(jax.random.fold_in(own_key, 6), dim), (shards_of,), jnp.float32, smallest / len(cuts), largest / len(cuts))
        level = level * jnp.repeat(jnp.exp(steps), shape[dim] // shards_of).reshape((-1,) + (1,) * (len(shape) - 1 - dim))
    return level


def normal_values(own_key, shape, width, bound, shards=(), dtype=jnp.bfloat16):
    factor_of = steps_of(own_key, shape, shards, -0.22, 0.18) if shards else 1.0
    values = jax.random.normal(own_key, shape, jnp.float32) * width * factor_of
    return jnp.minimum(jnp.maximum(values, -bound), bound).astype(dtype)


def setup_inputs(seed: int = 0) -> dict:
    arg_keys = jax.random.split(jax.random.key(seed), 4)
    source_terms = normal_values(arg_keys[0], (FIELDS, NZ, NR, NA), 1.0, 6.0, ((1, 4), (3, 64)), jnp.float32)
    diffusion = jnp.clip(jnp.exp(math.log(5.0) - 2.3025851 * jax.random.uniform(arg_keys[1], (FIELDS, NZ, NR, NA), jnp.float32) ** steps_of(arg_keys[1], (FIELDS, NZ, NR, NA), ((1, 4), (3, 64)), -0.2, 0.2)), 0.5, 5.0)
    mass_coefficient = jnp.clip(jnp.exp(math.log(50.0) - 2.3025851 * jax.random.uniform(arg_keys[2], (NZ, NR, NA), jnp.float32) ** steps_of(arg_keys[2], (NZ, NR, NA), ((0, 4), (2, 64)), -0.2, 0.2)), 5.0, 50.0)
    return dict(source_terms=source_terms, diffusion=diffusion, mass_coefficient=mass_coefficient)


def gll_tables():
    degree = 7
    points = np.array([-1.0, -0.8717401485096066, -0.5917001814331423, -0.2092992179024789, 0.2092992179024789, 0.5917001814331423, 0.8717401485096066, 1.0])
    previous = np.ones(degree + 1)
    current = points.copy()
    for order in range(1, degree):
        following = ((2 * order + 1) * points * current - order * previous) / (order + 1)
        previous = current
        current = following
    values = current
    weights = 2.0 / (degree * (degree + 1) * values * values)
    derivative = np.zeros((degree + 1, degree + 1))
    for first_index in range(degree + 1):
        for second_index in range(degree + 1):
            if first_index != second_index:
                derivative[first_index, second_index] = values[first_index] / (values[second_index] * (points[first_index] - points[second_index]))
    derivative[0, 0] = -degree * (degree + 1) / 4.0
    derivative[degree, degree] = degree * (degree + 1) / 4.0
    return weights, derivative


def apply_along(values, matrix, dimension):
    high = lax.Precision.HIGHEST
    shape_now = values.shape
    if dimension == 0:
        split = values.reshape(shape_now[0] // 8, 8, shape_now[1], shape_now[2])
        result = jnp.einsum('ji,eira->ejra', matrix, split, precision=high)
    elif dimension == 1:
        split = values.reshape(shape_now[0], shape_now[1] // 8, 8, shape_now[2])
        result = jnp.einsum('ji,zeia->zeja', matrix, split, precision=high)
    else:
        split = values.reshape(shape_now[0], shape_now[1], shape_now[2] // 8, 8)
        result = jnp.einsum('ji,zrei->zrej', matrix, split, precision=high)
    return result.reshape(shape_now)


def edge_masks(length, dimension):
    positions = jnp.arange(length) % 8
    shape_list = [1, 1, 1]
    shape_list[dimension] = length
    starts = (positions == 0).astype(jnp.float32).reshape(shape_list)
    finish = (positions == 7).astype(jnp.float32).reshape(shape_list)
    return starts, finish


def join_dimension(values, dimension, periodic):
    length = values.shape[dimension]
    if periodic:
        before = jnp.roll(values, 1, axis=dimension)
        after = jnp.roll(values, -1, axis=dimension)
    else:
        widths = [(0, 0), (0, 0), (0, 0)]
        widths[dimension] = (1, 1)
        padded = jnp.pad(values, widths)
        before = lax.slice_in_dim(padded, 0, length, axis=dimension)
        after = lax.slice_in_dim(padded, 2, length + 2, axis=dimension)
    starts, finish = edge_masks(length, dimension)
    return values + starts * before + finish * after


def summation(total):
    total = join_dimension(total, 2, True)
    total = join_dimension(total, 0, False)
    total = join_dimension(total, 1, False)
    return total


def multiplicity(length, periodic):
    positions = np.arange(length)
    shared = (positions % 8 == 0) | (positions % 8 == 7)
    if not periodic:
        shared = shared & (positions != 0) & (positions != length - 1)
    return np.where(shared, 2.0, 1.0)


def reference(source_terms, diffusion, mass_coefficient):
    weights, derivative = gll_tables()
    derivative_t = jnp.asarray(derivative, jnp.float32)
    transposed_t = jnp.asarray(derivative.T, jnp.float32)
    axial_len = source_terms.shape[1]
    radial_len = source_terms.shape[2]
    azimuth_len = source_terms.shape[3]
    weight_z = np.tile(weights, axial_len // 8).reshape(axial_len, 1, 1)
    weight_r = np.tile(weights, radial_len // 8).reshape(1, radial_len, 1)
    weight_a = np.tile(weights, azimuth_len // 8).reshape(1, 1, azimuth_len)
    quadrature = jnp.asarray(weight_z * weight_r * weight_a, jnp.float32)
    mult_z = multiplicity(axial_len, False).reshape(axial_len, 1, 1)
    mult_r = multiplicity(radial_len, False).reshape(1, radial_len, 1)
    mult_a = multiplicity(azimuth_len, True).reshape(1, 1, azimuth_len)
    inverse_mult = jnp.asarray(1.0 / (mult_z * mult_r * mult_a), jnp.float32)
    solutions = []
    residuals = []
    for moment in range(FIELDS):
        scaled = quadrature * diffusion[moment]
        massive = quadrature * mass_coefficient

        def operate(values):
            total = massive * values
            for dimension in range(3):
                gradient = apply_along(values, derivative_t, dimension)
                total = total + apply_along(scaled * gradient, transposed_t, dimension)
            return summation(total)

        def inner_product(left_side, right_side):
            return jnp.sum(left_side * right_side * inverse_mult)

        residual = summation(source_terms[moment])
        solution = jnp.zeros_like(residual)
        direction = residual
        norm_now = inner_product(residual, residual)
        for iteration in range(ITERS):
            applied = operate(direction)
            step_length = norm_now / inner_product(direction, applied)
            solution = solution + step_length * direction
            residual = residual - step_length * applied
            norm_next = inner_product(residual, residual)
            direction = residual + (norm_next / norm_now) * direction
            norm_now = norm_next
        solutions.append(solution)
        residuals.append(residual)
    return jnp.stack(solutions), jnp.stack(residuals)
```

```python
import jax
import jax.numpy as jnp
import numpy as np
from jax import lax
from jax.experimental import pallas as pl
from jax.experimental.pallas import tpu as pltpu
from jax.sharding import PartitionSpec as P

MESH = pl.DeviceIdType.MESH
FIELDS = 3
PHASES = 3
LANES = 128
TILES = 64


def gll_tables():
    degree = 7
    points = np.array(
        [
            -1.0,
            -0.8717401485096066,
            -0.5917001814331423,
            -0.2092992179024789,
            0.2092992179024789,
            0.5917001814331423,
            0.8717401485096066,
            1.0,
        ]
    )
    previous = np.ones(degree + 1)
    current = points.copy()
    for order in range(1, degree):
        following = ((2 * order + 1) * points * current - order * previous) / (order + 1)
        previous = current
        current = following
    weights = 2.0 / (degree * (degree + 1) * current * current)
    derivative = np.zeros((degree + 1, degree + 1))
    for first_index in range(degree + 1):
        for second_index in range(degree + 1):
            if first_index != second_index:
                derivative[first_index, second_index] = current[first_index] / (
                    current[second_index] * (points[first_index] - points[second_index])
                )
    derivative[0, 0] = -degree * (degree + 1) / 4.0
    derivative[degree, degree] = degree * (degree + 1) / 4.0
    return (weights, derivative)


WEIGHTS, DERIVATIVE = gll_tables()


def lane_operators():
    whole = np.kron(np.eye(LANES // 8), DERIVATIVE)
    return np.stack([whole.T, whole]).astype(np.float32)


def mix(matrix, values):
    even = [values[i] + values[7 - i] for i in range(4)]
    odd = [values[i] - values[7 - i] for i in range(4)]
    result = [None] * 8
    for j in range(4):
        from_even = None
        from_odd = None
        for i in range(4):
            a = float(0.5 * (matrix[j, i] + matrix[j, 7 - i])) * even[i]
            b = float(0.5 * (matrix[j, i] - matrix[j, 7 - i])) * odd[i]
            from_even = a if from_even is None else from_even + a
            from_odd = b if from_odd is None else from_odd + b
        result[j] = from_odd + from_even
        result[7 - j] = from_odd - from_even
    return result


def azi_shift(azi, axial, count):
    return lax.rem(azi + count + 64, 64), axial


def column_partner(azi, axial, index):
    z = lax.rem(azi, 8)
    other = azi - z + lax.rem(z + index // 2, 8)
    core = lax.rem(axial, 2)
    flipped = axial + (1 - 2 * core) if index % 2 else axial
    return other, flipped


def plane_partner(azi, axial, index):
    x = azi // 16
    y_hi = lax.rem(azi // 8, 2)
    z = lax.rem(azi, 8)
    x = lax.rem(x + index // 4, 4)
    y_hi = lax.rem(y_hi + (index // 2) % 2, 2)
    return x * 16 + y_hi * 8 + z, lax.rem(axial + 2 * (index % 2), 4)


def kernel(
    src_hbm,
    dif_hbm,
    mas_hbm,
    wts_hbm,
    sol,
    res,
    src,
    dif,
    mas,
    lane_ops,
    wts,
    scaled,
    massive,
    own,
    full,
    raw,
    packed,
    got_plane,
    got_packed,
    dots,
    ar_send,
    ar_got,
    in_sem,
    send_sem,
    recv_sem,
    ar_send_sem,
    ar_recv_sem,
):
    azi = lax.axis_index("azi")
    axial = lax.axis_index("axial")
    has_low = axial > 0
    has_high = axial < 3

    loads = []
    for f in range(FIELDS):
        loads.append(pltpu.make_async_copy(src_hbm.at[f], src.at[f], in_sem.at[f]))
    for f in range(FIELDS):
        loads.append(pltpu.make_async_copy(dif_hbm.at[f], dif.at[f], in_sem.at[3 + f]))
    loads.append(pltpu.make_async_copy(mas_hbm, mas, in_sem.at[6]))
    loads.append(pltpu.make_async_copy(wts_hbm, lane_ops, in_sem.at[7]))
    for copy in loads:
        copy.start()

    up = lax.rem(azi + 1, 64)
    down = lax.rem(azi + 63, 64)
    barrier = pltpu.get_barrier_semaphore()

    def greet(device):
        pl.semaphore_signal(barrier, inc=1, device_id=device, device_id_type=MESH)

    greet((up, axial))
    greet((down, axial))

    @pl.when(has_low)
    def _():
        for other in (up, azi, down):
            greet((other, axial - 1))

    @pl.when(has_high)
    def _():
        for other in (up, azi, down):
            greet((other, axial + 1))

    column = [column_partner(azi, axial, j) for j in range(1, 16)]
    plane = [plane_partner(azi, axial, j) for j in range(1, 16)]
    for device in column + plane:
        greet(device)

    @pl.when(jnp.logical_not(has_low))
    def _():
        for ph in range(PHASES):
            for f in range(FIELDS):
                got_plane[ph, f, 0] = jnp.zeros((8, 8, LANES), jnp.float32)
                got_packed[ph, f, 2] = jnp.zeros((8, LANES), jnp.float32)
                got_packed[ph, f, 3] = jnp.zeros((8, LANES), jnp.float32)

    @pl.when(jnp.logical_not(has_high))
    def _():
        for ph in range(PHASES):
            for f in range(FIELDS):
                got_plane[ph, f, 1] = jnp.zeros((8, 8, LANES), jnp.float32)
                got_packed[ph, f, 4] = jnp.zeros((8, LANES), jnp.float32)
                got_packed[ph, f, 5] = jnp.zeros((8, LANES), jnp.float32)

    lane = lax.broadcasted_iota(jnp.int32, (8, LANES), 1)
    sub = lax.broadcasted_iota(jnp.int32, (8, LANES), 0)
    in_element = lane % 8
    starts = (in_element == 0) & (lane != 0)
    finish = (in_element == 7) & (lane != LANES - 1)
    outer = (lane == 0) | (lane == LANES - 1)
    even_lane = lane % 2 == 0
    group_of_lane = ((lane + 1) % LANES) // 16
    pair_of_lane = ((lane + 1) % LANES) // 2
    zeros = jnp.zeros((8, LANES), jnp.float32)

    def join_lanes(tile):
        before = pltpu.roll(tile, 1, 1)
        after = pltpu.roll(tile, LANES - 1, 1)
        return tile + jnp.where(starts, before, jnp.where(finish, after, 0.0))

    def join_rows(tiles):
        first, last = tiles[0], tiles[7]
        tiles[0] = first + jnp.where(sub > 0, pltpu.roll(last, 1, 0), 0.0)
        tiles[7] = last + jnp.where(sub < 7, pltpu.roll(first, 7, 0), 0.0)
        return tiles

    def assemble_own(ph, f, z, tiles, faces):
        tiles = join_rows(list(tiles))
        line = zeros
        for i in range(8):
            tile = join_lanes(tiles[i])
            own[ph, f, z * 8 + i] = tile
            turned = pltpu.roll(tile, 2 * i, 1) if i else tile
            line = jnp.where(pair_of_lane == i, turned, line)
        return jnp.where(group_of_lane == z, pltpu.roll(line, z * 16, 1), faces)

    def copies(ph, f):
        def remote(source, target, slot, device):
            return pltpu.make_async_remote_copy(
                src_ref=source,
                dst_ref=target,
                send_sem=send_sem.at[ph, f, slot],
                recv_sem=recv_sem.at[ph, f, slot],
                device_id=device,
                device_id_type=MESH,
            )

        tile = packed.at[ph, f]
        slots = got_packed.at[ph, f]
        always = [
            remote(tile, slots.at[0], 0, (up, axial)),
            remote(tile, slots.at[1], 1, (down, axial)),
        ]
        above = [
            remote(tile, slots.at[2], 2, (up, axial + 1)),
            remote(tile, slots.at[3], 3, (down, axial + 1)),
            remote(own.at[ph, f, pl.ds(56, 8)], got_plane.at[ph, f, 0], 6, (azi, axial + 1)),
        ]
        below = [
            remote(tile, slots.at[4], 4, (up, axial - 1)),
            remote(tile, slots.at[5], 5, (down, axial - 1)),
            remote(own.at[ph, f, pl.ds(0, 8)], got_plane.at[ph, f, 1], 7, (azi, axial - 1)),
        ]
        return always, above, below

    def send(ph, f):
        always, above, below = copies(ph, f)
        for copy in always:
            copy.start()

        @pl.when(has_high)
        def _():
            for copy in above:
                copy.start()

        @pl.when(has_low)
        def _():
            for copy in below:
                copy.start()

    def receive(ph, f):
        always, above, below = copies(ph, f)
        for copy in always:
            copy.wait_recv()

        @pl.when(has_low)
        def _():
            for copy in above:
                copy.wait_recv()

        @pl.when(has_high)
        def _():
            for copy in below:
                copy.wait_recv()

    def finish_sends(ph, f):
        always, above, below = copies(ph, f)
        for copy in always:
            copy.wait_send()

        @pl.when(has_high)
        def _():
            for copy in above:
                copy.wait_send()

        @pl.when(has_low)
        def _():
            for copy in below:
                copy.wait_send()

    def complete(ph, f, use, carry):
        receive(ph, f)

        def faced(left, right):
            return jnp.where(
                even_lane, pltpu.roll(left, 1, 1), pltpu.roll(right, LANES - 1, 1)
            )

        slots = [got_packed[ph, f, s] for s in range(6)]
        faces = faced(slots[0], slots[1])
        low = pltpu.roll(faced(slots[2], slots[3]), LANES - 112, 1)
        high = pltpu.roll(faced(slots[4], slots[5]), 112, 1)
        faces = faces + jnp.where(group_of_lane == 0, low, 0.0)
        faces = faces + jnp.where(group_of_lane == 7, high, 0.0)

        def one(z, carry, plane):
            line = pltpu.roll(faces, lax.rem(LANES - z * 16, LANES), 1)
            for i in range(8):
                turned = pltpu.roll(line, LANES - 2 * i, 1) if i else line
                tile = own[ph, f, z * 8 + i] + jnp.where(outer, turned, 0.0)
                if plane is not None:
                    tile = tile + got_plane[ph, f, plane, i]
                carry = use(z, i, tile, carry)
            return carry

        carry = one(0, carry, 0)
        carry = lax.fori_loop(1, 7, lambda z, c: one(z, c, None), carry)
        return one(7, carry, 1)

    def split_dot(values, which):
        high = values.astype(jnp.bfloat16)
        low = (values - high.astype(jnp.float32)).astype(jnp.bfloat16)
        both = jnp.dot(
            jnp.concatenate([high, low], axis=1), wts[which], preferred_element_type=jnp.float32
        )
        return both[:, :LANES] + both[:, LANES:]

    def operate(k, f):
        values = full[k, f].reshape(TILES * 8, LANES)
        gradient = split_dot(values, 0) * scaled[f].reshape(TILES * 8, LANES)
        raw[f] = split_dot(gradient, 1).reshape(TILES, 8, LANES)

        def along_axial(i, carry):
            tiles = [full[k, f, z * 8 + i] for z in range(8)]
            gradient = mix(DERIVATIVE, tiles)
            gradient = [scaled[f, z * 8 + i] * gradient[z] for z in range(8)]
            back = mix(DERIVATIVE.T, gradient)
            for z in range(8):
                raw[f, z * 8 + i] = raw[f, z * 8 + i] + (back[z] + massive[z * 8 + i] * tiles[z])
            return carry

        lax.fori_loop(0, 8, along_axial, 0)

        def along_radius(z, carry):
            total, faces = carry
            tiles = [full[k, f, z * 8 + i] for i in range(8)]
            gradient = mix(DERIVATIVE, tiles)
            gradient = [scaled[f, z * 8 + i] * gradient[i] for i in range(8)]
            back = mix(DERIVATIVE.T, gradient)
            back = [raw[f, z * 8 + i] + back[i] for i in range(8)]
            for i in range(8):
                total = total + tiles[i] * back[i]
                raw[f, z * 8 + i] = back[i]
            return total, assemble_own(k + 1, f, z, back, faces)

        total, faces = lax.fori_loop(0, 8, along_radius, (zeros, zeros))
        packed[k + 1, f] = faces
        return total

    def native(ref, f, z, i):
        return ref[f, z, pl.ds(i, 8, stride=8), :]

    for f in range(FIELDS):
        loads[f].wait()

        def gather(z, faces):
            return assemble_own(0, f, z, [native(src, f, z, i) for i in range(8)], faces)

        packed[0, f] = lax.fori_loop(0, 8, gather, zeros)

    around = axial * 0 + 2 + 30 + jnp.where(has_low, 3, 0) + jnp.where(has_high, 3, 0)
    pl.semaphore_wait(barrier, around)
    for f in range(FIELDS):
        send(0, f)

    weight_a = jnp.zeros((8, LANES), jnp.float32)
    for i in range(8):
        weight_a = jnp.where(in_element == i, float(WEIGHTS[i]), weight_a)
    loads[6].wait()
    for f in range(FIELDS):
        loads[3 + f].wait()
    loads[7].wait()
    for which in range(2):
        high = lane_ops[which].astype(jnp.bfloat16)
        low = (lane_ops[which] - high.astype(jnp.float32)).astype(jnp.bfloat16)
        wts[which, :LANES, :LANES] = high
        wts[which, :LANES, LANES:] = low
        wts[which, LANES:, :LANES] = high
        wts[which, LANES:, LANES:] = jnp.zeros((LANES, LANES), jnp.bfloat16)
    for z in range(8):
        for i in range(8):
            weight = float(WEIGHTS[z] * WEIGHTS[i]) * weight_a
            massive[z * 8 + i] = weight * mas[z, pl.ds(i, 8, stride=8), :]
            for f in range(FIELDS):
                scaled[f, z * 8 + i] = weight * native(dif, f, z, i)

    for f in range(FIELDS):

        def keep_rhs(z, i, tile, total):
            full[0, f, z * 8 + i] = tile
            return total + tile * native(src, f, z, i)

        dots[f] = complete(0, f, keep_rhs, zeros)
        dots[3 + f] = operate(0, f)
        send(1, f)

    for f in range(FIELDS):

        def keep_image(z, i, tile, total):
            full[1, f, z * 8 + i] = tile
            return total + tile * raw[f, z * 8 + i]

        dots[6 + f] = complete(1, f, keep_image, zeros)
        dots[9 + f] = operate(1, f)
        send(2, f)

    lane_row = lax.broadcasted_iota(jnp.int32, (1, LANES), 1)
    row = jnp.zeros((1, LANES), jnp.float32)
    for j in range(12):
        part = jnp.sum(jnp.sum(dots[j], axis=0, keepdims=True), axis=1, keepdims=True)
        row = jnp.where(lane_row == j, part, row)

    def exchange(stage, partners, row):
        ar_send[stage] = row
        sent = []
        for j, device in enumerate(partners):
            copy = pltpu.make_async_remote_copy(
                src_ref=ar_send.at[stage],
                dst_ref=ar_got.at[stage, j],
                send_sem=ar_send_sem.at[stage, j],
                recv_sem=ar_recv_sem.at[stage, j],
                device_id=device,
                device_id_type=MESH,
            )
            copy.start()
            sent.append(copy)
        return sent

    def gathered(stage, sent, row):
        for copy in sent:
            copy.wait_recv()
        return row + jnp.sum(ar_got[stage], axis=0)

    first = exchange(0, column, row)
    row = gathered(0, first, row)
    second = exchange(1, plane, row)

    for f in range(FIELDS):

        def keep_second(z, i, tile, carry):
            raw[f, z * 8 + i] = tile
            return carry

        complete(2, f, keep_second, 0)

    row = gathered(1, second, row)

    def moved(count):
        return pltpu.roll(jnp.broadcast_to(row, (8, LANES)), LANES - count, 1)

    norm = jnp.where(lane < FIELDS, jnp.broadcast_to(row, (8, LANES)), 1.0)
    beta = moved(3) / norm
    gamma = moved(6) / norm
    delta = moved(9) / norm
    below = beta * delta - gamma * gamma
    below = jnp.where(lane < FIELDS, below, 1.0)
    one_image = (delta - beta * gamma) / below
    two_images = (gamma - beta * beta) / below

    for f in range(FIELDS):
        c = jnp.broadcast_to(one_image[:, f : f + 1], (8, LANES))
        d = jnp.broadcast_to(two_images[:, f : f + 1], (8, LANES))

        def combine(z, carry):
            for i in range(8):
                rhs = full[0, f, z * 8 + i]
                image = full[1, f, z * 8 + i]
                twice = raw[f, z * 8 + i]
                sol[f, z, pl.ds(i, 8, stride=8), :] = c * rhs - d * image
                res[f, z, pl.ds(i, 8, stride=8), :] = rhs - c * image + d * twice
            return carry

        lax.fori_loop(0, 8, combine, 0)

    for copy in first + second:
        copy.wait_send()
    for ph in range(PHASES):
        for f in range(FIELDS):
            finish_sends(ph, f)


def shards(source_terms, diffusion, mass_coefficient):
    shape = source_terms.shape
    field = (FIELDS, TILES, 8, LANES)
    f32 = jnp.float32
    operators = jnp.asarray(lane_operators())
    return pl.pallas_call(
        kernel,
        out_shape=(jax.ShapeDtypeStruct(shape, f32), jax.ShapeDtypeStruct(shape, f32)),
        in_specs=[pl.BlockSpec(memory_space=pltpu.HBM)] * 4,
        out_specs=(
            pl.BlockSpec(memory_space=pltpu.VMEM),
            pl.BlockSpec(memory_space=pltpu.VMEM),
        ),
        scratch_shapes=[
            pltpu.VMEM(shape, f32),
            pltpu.VMEM(shape, f32),
            pltpu.VMEM(mass_coefficient.shape, f32),
            pltpu.VMEM((2, LANES, LANES), f32),
            pltpu.VMEM((2, 2 * LANES, 2 * LANES), jnp.bfloat16),
            pltpu.VMEM(field, f32),
            pltpu.VMEM(field[1:], f32),
            pltpu.VMEM((PHASES,) + field, f32),
            pltpu.VMEM((2,) + field, f32),
            pltpu.VMEM(field, f32),
            pltpu.VMEM((PHASES, FIELDS, 8, LANES), f32),
            pltpu.VMEM((PHASES, FIELDS, 2, 8, 8, LANES), f32),
            pltpu.VMEM((PHASES, FIELDS, 6, 8, LANES), f32),
            pltpu.VMEM((12, 8, LANES), f32),
            pltpu.VMEM((2, 1, LANES), f32),
            pltpu.VMEM((2, 15, 1, LANES), f32),
            pltpu.SemaphoreType.DMA((8,)),
            pltpu.SemaphoreType.DMA((PHASES, FIELDS, 8)),
            pltpu.SemaphoreType.DMA((PHASES, FIELDS, 8)),
            pltpu.SemaphoreType.DMA((2, 15)),
            pltpu.SemaphoreType.DMA((2, 15)),
        ],
        compiler_params=pltpu.CompilerParams(
            collective_id=0, has_side_effects=True, vmem_limit_bytes=40 * 1024 * 1024
        ),
    )(source_terms, diffusion, mass_coefficient, operators)


def solution(mesh):
    in_specs = (
        P(None, "axial", None, "azi"),
        P(None, "axial", None, "azi"),
        P("axial", None, "azi"),
    )
    out_specs = (P(None, "axial", None, "azi"), P(None, "axial", None, "azi"))
    return jax.shard_map(shards, mesh=mesh, in_specs=in_specs, out_specs=out_specs, check_vma=False)
```

```python
import jax
import jax.numpy as jnp
import numpy as np
from jax import lax
from jax.experimental import pallas as pl
from jax.experimental.pallas import tpu as pltpu
from jax.sharding import PartitionSpec as P

MESH = pl.DeviceIdType.MESH
FIELDS = 3
PHASES = 3
LANES = 128
TILES = 64


def gll_tables():
    degree = 7
    points = np.array(
        [
            -1.0,
            -0.8717401485096066,
            -0.5917001814331423,
            -0.2092992179024789,
            0.2092992179024789,
            0.5917001814331423,
            0.8717401485096066,
            1.0,
        ]
    )
    previous = np.ones(degree + 1)
    current = points.copy()
    for order in range(1, degree):
        following = ((2 * order + 1) * points * current - order * previous) / (order + 1)
        previous = current
        current = following
    weights = 2.0 / (degree * (degree + 1) * current * current)
    derivative = np.zeros((degree + 1, degree + 1))
    for first_index in range(degree + 1):
        for second_index in range(degree + 1):
            if first_index != second_index:
                derivative[first_index, second_index] = current[first_index] / (
                    current[second_index] * (points[first_index] - points[second_index])
                )
    derivative[0, 0] = -degree * (degree + 1) / 4.0
    derivative[degree, degree] = degree * (degree + 1) / 4.0
    return (weights, derivative)


WEIGHTS, DERIVATIVE = gll_tables()


def lane_operators():
    whole = np.kron(np.eye(LANES // 8), DERIVATIVE)
    return np.stack([whole.T, whole]).astype(np.float32)


def mix(matrix, values):
    even = [values[i] + values[7 - i] for i in range(4)]
    odd = [values[i] - values[7 - i] for i in range(4)]
    result = [None] * 8
    for j in range(4):
        from_even = None
        from_odd = None
        for i in range(4):
            a = float(0.5 * (matrix[j, i] + matrix[j, 7 - i])) * even[i]
            b = float(0.5 * (matrix[j, i] - matrix[j, 7 - i])) * odd[i]
            from_even = a if from_even is None else from_even + a
            from_odd = b if from_odd is None else from_odd + b
        result[j] = from_odd + from_even
        result[7 - j] = from_odd - from_even
    return result


def azi_shift(azi, axial, count):
    return lax.rem(azi + count + 64, 64), axial


def column_partner(azi, axial, index):
    z = lax.rem(azi, 8)
    other = azi - z + lax.rem(z + index // 2, 8)
    core = lax.rem(axial, 2)
    flipped = axial + (1 - 2 * core) if index % 2 else axial
    return other, flipped


def plane_partner(azi, axial, index):
    x = azi // 16
    y_hi = lax.rem(azi // 8, 2)
    z = lax.rem(azi, 8)
    x = lax.rem(x + index // 4, 4)
    y_hi = lax.rem(y_hi + (index // 2) % 2, 2)
    return x * 16 + y_hi * 8 + z, lax.rem(axial + 2 * (index % 2), 4)


def kernel(
    src_hbm,
    dif_hbm,
    mas_hbm,
    wts_hbm,
    sol,
    res,
    src,
    dif,
    mas,
    lane_ops,
    wts,
    scaled,
    massive,
    own,
    full,
    raw,
    packed,
    got_plane,
    got_packed,
    dots,
    ar_send,
    ar_got,
    in_sem,
    send_sem,
    recv_sem,
    ar_send_sem,
    ar_recv_sem,
):
    azi = lax.axis_index("azi")
    axial = lax.axis_index("axial")
    has_low = axial > 0
    has_high = axial < 3

    loads = []
    for f in range(FIELDS):
        loads.append(pltpu.make_async_copy(src_hbm.at[f], src.at[f], in_sem.at[f]))
    for f in range(FIELDS):
        loads.append(pltpu.make_async_copy(dif_hbm.at[f], dif.at[f], in_sem.at[3 + f]))
    loads.append(pltpu.make_async_copy(mas_hbm, mas, in_sem.at[6]))
    loads.append(pltpu.make_async_copy(wts_hbm, lane_ops, in_sem.at[7]))
    for copy in loads:
        copy.start()

    up = lax.rem(azi + 1, 64)
    down = lax.rem(azi + 63, 64)
    barrier = pltpu.get_barrier_semaphore()

    def greet(device):
        pl.semaphore_signal(barrier, inc=1, device_id=device, device_id_type=MESH)

    greet((up, axial))
    greet((down, axial))

    @pl.when(has_low)
    def _():
        for other in (up, azi, down):
            greet((other, axial - 1))

    @pl.when(has_high)
    def _():
        for other in (up, azi, down):
            greet((other, axial + 1))

    column = [column_partner(azi, axial, j) for j in range(1, 16)]
    plane = [plane_partner(azi, axial, j) for j in range(1, 16)]
    for device in column + plane:
        greet(device)

    @pl.when(jnp.logical_not(has_low))
    def _():
        for ph in range(PHASES):
            for f in range(FIELDS):
                got_plane[ph, f, 0] = jnp.zeros((8, 8, LANES), jnp.float32)
                got_packed[ph, f, 2] = jnp.zeros((8, LANES), jnp.float32)
                got_packed[ph, f, 3] = jnp.zeros((8, LANES), jnp.float32)

    @pl.when(jnp.logical_not(has_high))
    def _():
        for ph in range(PHASES):
            for f in range(FIELDS):
                got_plane[ph, f, 1] = jnp.zeros((8, 8, LANES), jnp.float32)
                got_packed[ph, f, 4] = jnp.zeros((8, LANES), jnp.float32)
                got_packed[ph, f, 5] = jnp.zeros((8, LANES), jnp.float32)

    lane = lax.broadcasted_iota(jnp.int32, (8, LANES), 1)
    sub = lax.broadcasted_iota(jnp.int32, (8, LANES), 0)
    in_element = lane % 8
    starts = (in_element == 0) & (lane != 0)
    finish = (in_element == 7) & (lane != LANES - 1)
    outer = (lane == 0) | (lane == LANES - 1)
    even_lane = lane % 2 == 0
    group_of_lane = ((lane + 1) % LANES) // 16
    pair_of_lane = ((lane + 1) % LANES) // 2
    zeros = jnp.zeros((8, LANES), jnp.float32)

    def join_lanes(tile):
        before = pltpu.roll(tile, 1, 1)
        after = pltpu.roll(tile, LANES - 1, 1)
        return tile + jnp.where(starts, before, jnp.where(finish, after, 0.0))

    def join_rows(tiles):
        first, last = tiles[0], tiles[7]
        tiles[0] = first + jnp.where(sub > 0, pltpu.roll(last, 1, 0), 0.0)
        tiles[7] = last + jnp.where(sub < 7, pltpu.roll(first, 7, 0), 0.0)
        return tiles

    def assemble_own(ph, f, z, tiles, faces):
        tiles = join_rows(list(tiles))
        line = zeros
        for i in range(8):
            tile = join_lanes(tiles[i])
            own[ph, f, z * 8 + i] = tile
            turned = pltpu.roll(tile, 2 * i, 1) if i else tile
            line = jnp.where(pair_of_lane == i, turned, line)
        return jnp.where(group_of_lane == z, pltpu.roll(line, z * 16, 1) if z else line, faces)

    def copies(ph, f):
        def remote(source, target, slot, device):
            return pltpu.make_async_remote_copy(
                src_ref=source,
                dst_ref=target,
                send_sem=send_sem.at[ph, f, slot],
                recv_sem=recv_sem.at[ph, f, slot],
                device_id=device,
                device_id_type=MESH,
            )

        tile = packed.at[ph, f]
        slots = got_packed.at[ph, f]
        always = [
            remote(tile, slots.at[0], 0, (up, axial)),
            remote(tile, slots.at[1], 1, (down, axial)),
        ]
        above = [
            remote(tile, slots.at[2], 2, (up, axial + 1)),
            remote(tile, slots.at[3], 3, (down, axial + 1)),
            remote(own.at[ph, f, pl.ds(56, 8)], got_plane.at[ph, f, 0], 6, (azi, axial + 1)),
        ]
        below = [
            remote(tile, slots.at[4], 4, (up, axial - 1)),
            remote(tile, slots.at[5], 5, (down, axial - 1)),
            remote(own.at[ph, f, pl.ds(0, 8)], got_plane.at[ph, f, 1], 7, (azi, axial - 1)),
        ]
        return always, above, below

    def send(ph, f):
        always, above, below = copies(ph, f)
        for copy in always:
            copy.start()

        @pl.when(has_high)
        def _():
            for copy in above:
                copy.start()

        @pl.when(has_low)
        def _():
            for copy in below:
                copy.start()

    def receive(ph, f):
        always, above, below = copies(ph, f)
        for copy in always:
            copy.wait_recv()

        @pl.when(has_low)
        def _():
            for copy in above:
                copy.wait_recv()

        @pl.when(has_high)
        def _():
            for copy in below:
                copy.wait_recv()

    def finish_sends(ph, f):
        always, above, below = copies(ph, f)
        for copy in always:
            copy.wait_send()

        @pl.when(has_high)
        def _():
            for copy in above:
                copy.wait_send()

        @pl.when(has_low)
        def _():
            for copy in below:
                copy.wait_send()

    def complete(ph, f, use, carry):
        receive(ph, f)

        def faced(left, right):
            return jnp.where(
                even_lane, pltpu.roll(left, 1, 1), pltpu.roll(right, LANES - 1, 1)
            )

        slots = [got_packed[ph, f, s] for s in range(6)]
        faces = faced(slots[0], slots[1])
        low = pltpu.roll(faced(slots[2], slots[3]), LANES - 112, 1)
        high = pltpu.roll(faced(slots[4], slots[5]), 112, 1)
        faces = faces + jnp.where(group_of_lane == 0, low, 0.0)
        faces = faces + jnp.where(group_of_lane == 7, high, 0.0)

        def one(z, carry, plane):
            line = pltpu.roll(faces, LANES - z * 16, 1) if z else faces
            for i in range(8):
                turned = pltpu.roll(line, LANES - 2 * i, 1) if i else line
                tile = own[ph, f, z * 8 + i] + jnp.where(outer, turned, 0.0)
                if plane is not None:
                    tile = tile + got_plane[ph, f, plane, i]
                carry = use(z, i, tile, carry)
            return carry

        carry = one(0, carry, 0)
        for z in range(1, 7):
            carry = one(z, carry, None)
        return one(7, carry, 1)

    def split_dot(values, which):
        high = values.astype(jnp.bfloat16)
        low = (values - high.astype(jnp.float32)).astype(jnp.bfloat16)
        both = jnp.dot(
            jnp.concatenate([high, low], axis=1), wts[which], preferred_element_type=jnp.float32
        )
        return both[:, :LANES] + both[:, LANES:]

    def operate(k, f):
        values = full[k, f].reshape(TILES * 8, LANES)
        gradient = split_dot(values, 0) * scaled[f].reshape(TILES * 8, LANES)
        raw[f] = split_dot(gradient, 1).reshape(TILES, 8, LANES)

        def along_axial(i, carry):
            tiles = [full[k, f, z * 8 + i] for z in range(8)]
            gradient = mix(DERIVATIVE, tiles)
            gradient = [scaled[f, z * 8 + i] * gradient[z] for z in range(8)]
            back = mix(DERIVATIVE.T, gradient)
            for z in range(8):
                raw[f, z * 8 + i] = raw[f, z * 8 + i] + (back[z] + massive[z * 8 + i] * tiles[z])
            return carry

        for i in range(8):
            along_axial(i, 0)

        def along_radius(z, carry):
            total, faces = carry
            tiles = [full[k, f, z * 8 + i] for i in range(8)]
            gradient = mix(DERIVATIVE, tiles)
            gradient = [scaled[f, z * 8 + i] * gradient[i] for i in range(8)]
            back = mix(DERIVATIVE.T, gradient)
            back = [raw[f, z * 8 + i] + back[i] for i in range(8)]
            for i in range(8):
                total = total + tiles[i] * back[i]
                raw[f, z * 8 + i] = back[i]
            return total, assemble_own(k + 1, f, z, back, faces)

        total, faces = zeros, zeros
        for z in range(8):
            total, faces = along_radius(z, (total, faces))
        packed[k + 1, f] = faces
        return total

    def native(ref, f, z, i):
        return ref[f, z, pl.ds(i, 8, stride=8), :]

    for f in range(FIELDS):
        loads[f].wait()

        def gather(z, faces):
            return assemble_own(0, f, z, [native(src, f, z, i) for i in range(8)], faces)

        faces = zeros
        for z in range(8):
            faces = gather(z, faces)
        packed[0, f] = faces

    around = axial * 0 + 2 + 30 + jnp.where(has_low, 3, 0) + jnp.where(has_high, 3, 0)
    pl.semaphore_wait(barrier, around)
    for f in range(FIELDS):
        send(0, f)

    weight_a = jnp.zeros((8, LANES), jnp.float32)
    for i in range(8):
        weight_a = jnp.where(in_element == i, float(WEIGHTS[i]), weight_a)
    loads[6].wait()
    for f in range(FIELDS):
        loads[3 + f].wait()
    loads[7].wait()
    for which in range(2):
        high = lane_ops[which].astype(jnp.bfloat16)
        low = (lane_ops[which] - high.astype(jnp.float32)).astype(jnp.bfloat16)
        wts[which, :LANES, :LANES] = high
        wts[which, :LANES, LANES:] = low
        wts[which, LANES:, :LANES] = high
        wts[which, LANES:, LANES:] = jnp.zeros((LANES, LANES), jnp.bfloat16)
    for z in range(8):
        for i in range(8):
            weight = float(WEIGHTS[z] * WEIGHTS[i]) * weight_a
            massive[z * 8 + i] = weight * mas[z, pl.ds(i, 8, stride=8), :]
            for f in range(FIELDS):
                scaled[f, z * 8 + i] = weight * native(dif, f, z, i)

    for f in range(FIELDS):

        def keep_rhs(z, i, tile, total):
            full[0, f, z * 8 + i] = tile
            return total + tile * native(src, f, z, i)

        dots[f] = complete(0, f, keep_rhs, zeros)
        dots[3 + f] = operate(0, f)
        send(1, f)

    for f in range(FIELDS):

        def keep_image(z, i, tile, total):
            full[1, f, z * 8 + i] = tile
            return total + tile * raw[f, z * 8 + i]

        dots[6 + f] = complete(1, f, keep_image, zeros)
        dots[9 + f] = operate(1, f)
        send(2, f)

    lane_row = lax.broadcasted_iota(jnp.int32, (1, LANES), 1)
    row = jnp.zeros((1, LANES), jnp.float32)
    for j in range(12):
        part = jnp.sum(jnp.sum(dots[j], axis=0, keepdims=True), axis=1, keepdims=True)
        row = jnp.where(lane_row == j, part, row)

    def exchange(stage, partners, row):
        ar_send[stage] = row
        sent = []
        for j, device in enumerate(partners):
            copy = pltpu.make_async_remote_copy(
                src_ref=ar_send.at[stage],
                dst_ref=ar_got.at[stage, j],
                send_sem=ar_send_sem.at[stage, j],
                recv_sem=ar_recv_sem.at[stage, j],
                device_id=device,
                device_id_type=MESH,
            )
            copy.start()
            sent.append(copy)
        return sent

    def gathered(stage, sent, row):
        for copy in sent:
            copy.wait_recv()
        return row + jnp.sum(ar_got[stage], axis=0)

    first = exchange(0, column, row)
    row = gathered(0, first, row)
    second = exchange(1, plane, row)

    for f in range(FIELDS):

        def keep_second(z, i, tile, carry):
            raw[f, z * 8 + i] = tile
            return carry

        complete(2, f, keep_second, 0)

    row = gathered(1, second, row)

    def moved(count):
        return pltpu.roll(jnp.broadcast_to(row, (8, LANES)), LANES - count, 1)

    norm = jnp.where(lane < FIELDS, jnp.broadcast_to(row, (8, LANES)), 1.0)
    beta = moved(3) / norm
    gamma = moved(6) / norm
    delta = moved(9) / norm
    below = beta * delta - gamma * gamma
    below = jnp.where(lane < FIELDS, below, 1.0)
    one_image = (delta - beta * gamma) / below
    two_images = (gamma - beta * beta) / below

    for f in range(FIELDS):
        c = jnp.broadcast_to(one_image[:, f : f + 1], (8, LANES))
        d = jnp.broadcast_to(two_images[:, f : f + 1], (8, LANES))

        def combine(z, carry):
            for i in range(8):
                rhs = full[0, f, z * 8 + i]
                image = full[1, f, z * 8 + i]
                twice = raw[f, z * 8 + i]
                sol[f, z, pl.ds(i, 8, stride=8), :] = c * rhs - d * image
                res[f, z, pl.ds(i, 8, stride=8), :] = rhs - c * image + d * twice
            return carry

        for z in range(8):
            combine(z, 0)

    for copy in first + second:
        copy.wait_send()
    for ph in range(PHASES):
        for f in range(FIELDS):
            finish_sends(ph, f)


def shards(source_terms, diffusion, mass_coefficient):
    shape = source_terms.shape
    field = (FIELDS, TILES, 8, LANES)
    f32 = jnp.float32
    operators = jnp.asarray(lane_operators())
    return pl.pallas_call(
        kernel,
        out_shape=(jax.ShapeDtypeStruct(shape, f32), jax.ShapeDtypeStruct(shape, f32)),
        in_specs=[pl.BlockSpec(memory_space=pltpu.HBM)] * 4,
        out_specs=(
            pl.BlockSpec(memory_space=pltpu.VMEM),
            pl.BlockSpec(memory_space=pltpu.VMEM),
        ),
        scratch_shapes=[
            pltpu.VMEM(shape, f32),
            pltpu.VMEM(shape, f32),
            pltpu.VMEM(mass_coefficient.shape, f32),
            pltpu.VMEM((2, LANES, LANES), f32),
            pltpu.VMEM((2, 2 * LANES, 2 * LANES), jnp.bfloat16),
            pltpu.VMEM(field, f32),
            pltpu.VMEM(field[1:], f32),
            pltpu.VMEM((PHASES,) + field, f32),
            pltpu.VMEM((2,) + field, f32),
            pltpu.VMEM(field, f32),
            pltpu.VMEM((PHASES, FIELDS, 8, LANES), f32),
            pltpu.VMEM((PHASES, FIELDS, 2, 8, 8, LANES), f32),
            pltpu.VMEM((PHASES, FIELDS, 6, 8, LANES), f32),
            pltpu.VMEM((12, 8, LANES), f32),
            pltpu.VMEM((2, 1, LANES), f32),
            pltpu.VMEM((2, 15, 1, LANES), f32),
            pltpu.SemaphoreType.DMA((8,)),
            pltpu.SemaphoreType.DMA((PHASES, FIELDS, 8)),
            pltpu.SemaphoreType.DMA((PHASES, FIELDS, 8)),
            pltpu.SemaphoreType.DMA((2, 15)),
            pltpu.SemaphoreType.DMA((2, 15)),
        ],
        compiler_params=pltpu.CompilerParams(
            collective_id=0, has_side_effects=True, vmem_limit_bytes=40 * 1024 * 1024
        ),
    )(*(pltpu.with_memory_space_constraint(x, pltpu.HBM) for x in (source_terms, diffusion, mass_coefficient, operators)))


def solution(mesh):
    in_specs = (
        P(None, "axial", None, "azi"),
        P(None, "axial", None, "azi"),
        P("axial", None, "azi"),
    )
    out_specs = (P(None, "axial", None, "azi"), P(None, "axial", None, "azi"))
    return jax.shard_map(shards, mesh=mesh, in_specs=in_specs, out_specs=out_specs, check_vma=False)
```

```python
import jax
import jax.numpy as jnp
import numpy as np
from jax import lax
from jax.experimental import pallas as pl
from jax.experimental.pallas import tpu as pltpu
from jax.sharding import PartitionSpec as P

MESH = pl.DeviceIdType.MESH
FIELDS = 3
PHASES = 3
PIECES = 1
LANES = 128
TILES = 64


def gll_tables():
    degree = 7
    points = np.array(
        [
            -1.0,
            -0.8717401485096066,
            -0.5917001814331423,
            -0.2092992179024789,
            0.2092992179024789,
            0.5917001814331423,
            0.8717401485096066,
            1.0,
        ]
    )
    previous = np.ones(degree + 1)
    current = points.copy()
    for order in range(1, degree):
        following = ((2 * order + 1) * points * current - order * previous) / (order + 1)
        previous = current
        current = following
    weights = 2.0 / (degree * (degree + 1) * current * current)
    derivative = np.zeros((degree + 1, degree + 1))
    for first_index in range(degree + 1):
        for second_index in range(degree + 1):
            if first_index != second_index:
                derivative[first_index, second_index] = current[first_index] / (
                    current[second_index] * (points[first_index] - points[second_index])
                )
    derivative[0, 0] = -degree * (degree + 1) / 4.0
    derivative[degree, degree] = degree * (degree + 1) / 4.0
    return (weights, derivative)


WEIGHTS, DERIVATIVE = gll_tables()


def lane_operators():
    whole = np.kron(np.eye(LANES // 8), DERIVATIVE)
    return np.stack([whole.T, whole]).astype(np.float32)


def mix(matrix, values):
    even = [values[i] + values[7 - i] for i in range(4)]
    odd = [values[i] - values[7 - i] for i in range(4)]
    result = [None] * 8
    for j in range(4):
        from_even = None
        from_odd = None
        for i in range(4):
            a = float(0.5 * (matrix[j, i] + matrix[j, 7 - i])) * even[i]
            b = float(0.5 * (matrix[j, i] - matrix[j, 7 - i])) * odd[i]
            from_even = a if from_even is None else from_even + a
            from_odd = b if from_odd is None else from_odd + b
        result[j] = from_odd + from_even
        result[7 - j] = from_odd - from_even
    return result


def azi_shift(azi, axial, count):
    return lax.rem(azi + count + 64, 64), axial


def column_partner(azi, axial, index):
    z = lax.rem(azi, 8)
    other = azi - z + lax.rem(z + index // 2, 8)
    core = lax.rem(axial, 2)
    flipped = axial + (1 - 2 * core) if index % 2 else axial
    return other, flipped


def plane_partner(azi, axial, index):
    x = azi // 16
    y_hi = lax.rem(azi // 8, 2)
    z = lax.rem(azi, 8)
    x = lax.rem(x + index // 4, 4)
    y_hi = lax.rem(y_hi + (index // 2) % 2, 2)
    return x * 16 + y_hi * 8 + z, lax.rem(axial + 2 * (index % 2), 4)


def kernel(
    src_hbm,
    dif_hbm,
    mas_hbm,
    wts_hbm,
    rhs_out,
    image_out,
    twice_out,
    coef_out,
    src,
    dif,
    mas,
    lane_ops,
    wts,
    scaled,
    massive,
    own,
    full,
    raw,
    packed,
    got_plane,
    got_packed,
    dots,
    ar_send,
    ar_got,
    in_sem,
    send_sem,
    recv_sem,
    ar_send_sem,
    ar_recv_sem,
):
    azi = lax.axis_index("azi")
    axial = lax.axis_index("axial")
    has_low = axial > 0
    has_high = axial < 3

    loads = []
    for f in range(FIELDS):
        loads.append(pltpu.make_async_copy(src_hbm.at[f], src.at[f], in_sem.at[f]))
    for f in range(FIELDS):
        loads.append(pltpu.make_async_copy(dif_hbm.at[f], dif.at[f], in_sem.at[3 + f]))
    loads.append(pltpu.make_async_copy(mas_hbm, mas, in_sem.at[6]))
    loads.append(pltpu.make_async_copy(wts_hbm, lane_ops, in_sem.at[7]))
    for copy in loads:
        copy.start()

    up = lax.rem(azi + 1, 64)
    down = lax.rem(azi + 63, 64)
    barrier = pltpu.get_barrier_semaphore()

    def greet(device):
        pl.semaphore_signal(barrier, inc=1, device_id=device, device_id_type=MESH)

    greet((up, axial))
    greet((down, axial))

    @pl.when(has_low)
    def _():
        for other in (up, azi, down):
            greet((other, axial - 1))

    @pl.when(has_high)
    def _():
        for other in (up, azi, down):
            greet((other, axial + 1))

    column = [column_partner(azi, axial, j) for j in range(1, 16)]
    plane = [plane_partner(azi, axial, j) for j in range(1, 16)]
    for device in column + plane:
        greet(device)

    @pl.when(jnp.logical_not(has_low))
    def _():
        for ph in range(PHASES):
            for f in range(FIELDS):
                got_plane[ph, f, 0] = jnp.zeros((8, 8, LANES), jnp.float32)
                got_packed[ph, f, 2] = jnp.zeros((8, LANES), jnp.float32)
                got_packed[ph, f, 3] = jnp.zeros((8, LANES), jnp.float32)

    @pl.when(jnp.logical_not(has_high))
    def _():
        for ph in range(PHASES):
            for f in range(FIELDS):
                got_plane[ph, f, 1] = jnp.zeros((8, 8, LANES), jnp.float32)
                got_packed[ph, f, 4] = jnp.zeros((8, LANES), jnp.float32)
                got_packed[ph, f, 5] = jnp.zeros((8, LANES), jnp.float32)

    lane = lax.broadcasted_iota(jnp.int32, (8, LANES), 1)
    sub = lax.broadcasted_iota(jnp.int32, (8, LANES), 0)
    in_element = lane % 8
    starts = (in_element == 0) & (lane != 0)
    finish = (in_element == 7) & (lane != LANES - 1)
    outer = (lane == 0) | (lane == LANES - 1)
    even_lane = lane % 2 == 0
    group_of_lane = ((lane + 1) % LANES) // 16
    pair_of_lane = ((lane + 1) % LANES) // 2
    zeros = jnp.zeros((8, LANES), jnp.float32)

    def join_lanes(tile):
        before = pltpu.roll(tile, 1, 1)
        after = pltpu.roll(tile, LANES - 1, 1)
        return tile + jnp.where(starts, before, jnp.where(finish, after, 0.0))

    def join_rows(tiles):
        first, last = tiles[0], tiles[7]
        tiles[0] = first + jnp.where(sub > 0, pltpu.roll(last, 1, 0), 0.0)
        tiles[7] = last + jnp.where(sub < 7, pltpu.roll(first, 7, 0), 0.0)
        return tiles

    def assemble_own(ph, f, z, tiles, faces):
        tiles = join_rows(list(tiles))
        line = zeros
        for i in range(8):
            tile = join_lanes(tiles[i])
            own[ph, f, z * 8 + i] = tile
            turned = pltpu.roll(tile, 2 * i, 1) if i else tile
            line = jnp.where(pair_of_lane == i, turned, line)
        return jnp.where(group_of_lane == z, pltpu.roll(line, z * 16, 1) if z else line, faces)

    def copies(ph, f):
        def remote(source, target, slot, device):
            return pltpu.make_async_remote_copy(
                src_ref=source,
                dst_ref=target,
                send_sem=send_sem.at[ph, f, slot],
                recv_sem=recv_sem.at[ph, f, slot],
                device_id=device,
                device_id_type=MESH,
            )

        tile = packed.at[ph, f]
        slots = got_packed.at[ph, f]
        always = [
            remote(tile, slots.at[0], 0, (up, axial)),
            remote(tile, slots.at[1], 1, (down, axial)),
        ]
        above = [
            remote(tile, slots.at[2], 2, (up, axial + 1)),
            remote(tile, slots.at[3], 3, (down, axial + 1)),
            remote(own.at[ph, f, pl.ds(56, 8)], got_plane.at[ph, f, 0], 6, (azi, axial + 1)),
        ]
        below = [
            remote(tile, slots.at[4], 4, (up, axial - 1)),
            remote(tile, slots.at[5], 5, (down, axial - 1)),
            remote(own.at[ph, f, pl.ds(0, 8)], got_plane.at[ph, f, 1], 7, (azi, axial - 1)),
        ]
        return always, above, below

    def send(ph, f):
        always, above, below = copies(ph, f)
        for copy in always:
            copy.start()

        @pl.when(has_high)
        def _():
            for copy in above:
                copy.start()

        @pl.when(has_low)
        def _():
            for copy in below:
                copy.start()

    def receive(ph, f):
        always, above, below = copies(ph, f)
        for copy in always:
            copy.wait_recv()

        @pl.when(has_low)
        def _():
            for copy in above:
                copy.wait_recv()

        @pl.when(has_high)
        def _():
            for copy in below:
                copy.wait_recv()

    def finish_sends(ph, f):
        always, above, below = copies(ph, f)
        for copy in always:
            copy.wait_send()

        @pl.when(has_high)
        def _():
            for copy in above:
                copy.wait_send()

        @pl.when(has_low)
        def _():
            for copy in below:
                copy.wait_send()

    def complete(ph, f, use, carry):
        receive(ph, f)

        def faced(left, right):
            return jnp.where(
                even_lane, pltpu.roll(left, 1, 1), pltpu.roll(right, LANES - 1, 1)
            )

        slots = [got_packed[ph, f, s] for s in range(6)]
        faces = faced(slots[0], slots[1])
        low = pltpu.roll(faced(slots[2], slots[3]), LANES - 112, 1)
        high = pltpu.roll(faced(slots[4], slots[5]), 112, 1)
        faces = faces + jnp.where(group_of_lane == 0, low, 0.0)
        faces = faces + jnp.where(group_of_lane == 7, high, 0.0)

        def one(z, carry, plane):
            line = pltpu.roll(faces, LANES - z * 16, 1) if z else faces
            for i in range(8):
                turned = pltpu.roll(line, LANES - 2 * i, 1) if i else line
                tile = own[ph, f, z * 8 + i] + jnp.where(outer, turned, 0.0)
                if plane is not None:
                    tile = tile + got_plane[ph, f, plane, i]
                carry = use(z, i, tile, carry)
            return carry

        carry = one(0, carry, 0)
        for z in range(1, 7):
            carry = one(z, carry, None)
        return one(7, carry, 1)

    def split_dot(values, which):
        high = values.astype(jnp.bfloat16)
        low = (values - high.astype(jnp.float32)).astype(jnp.bfloat16)
        both = jnp.dot(
            jnp.concatenate([high, low], axis=1), wts[which], preferred_element_type=jnp.float32
        )
        return both[:, :LANES] + both[:, LANES:]

    def operate(k, f):
        values = full[k, f].reshape(TILES * 8, LANES)
        gradient = split_dot(values, 0) * scaled[f].reshape(TILES * 8, LANES)
        raw[f] = split_dot(gradient, 1).reshape(TILES, 8, LANES)

        def along_axial(i, carry):
            tiles = [full[k, f, z * 8 + i] for z in range(8)]
            gradient = mix(DERIVATIVE, tiles)
            gradient = [scaled[f, z * 8 + i] * gradient[z] for z in range(8)]
            back = mix(DERIVATIVE.T, gradient)
            for z in range(8):
                raw[f, z * 8 + i] = raw[f, z * 8 + i] + (back[z] + massive[z * 8 + i] * tiles[z])
            return carry

        for i in range(8):
            along_axial(i, 0)

        def along_radius(z, carry):
            total, faces = carry
            tiles = [full[k, f, z * 8 + i] for i in range(8)]
            gradient = mix(DERIVATIVE, tiles)
            gradient = [scaled[f, z * 8 + i] * gradient[i] for i in range(8)]
            back = mix(DERIVATIVE.T, gradient)
            back = [raw[f, z * 8 + i] + back[i] for i in range(8)]
            for i in range(8):
                total = total + tiles[i] * back[i]
                raw[f, z * 8 + i] = back[i]
            return total, assemble_own(k + 1, f, z, back, faces)

        total, faces = zeros, zeros
        for z in range(8):
            total, faces = along_radius(z, (total, faces))
        packed[k + 1, f] = faces
        return total

    def native(ref, f, z, i):
        return ref[f, z, pl.ds(i, 8, stride=8), :]

    for f in range(FIELDS):
        loads[f].wait()

        def gather(z, faces):
            return assemble_own(0, f, z, [native(src, f, z, i) for i in range(8)], faces)

        faces = zeros
        for z in range(8):
            faces = gather(z, faces)
        packed[0, f] = faces

    around = axial * 0 + 2 + 30 + jnp.where(has_low, 3, 0) + jnp.where(has_high, 3, 0)
    pl.semaphore_wait(barrier, around)
    for f in range(FIELDS):
        send(0, f)

    weight_a = jnp.zeros((8, LANES), jnp.float32)
    for i in range(8):
        weight_a = jnp.where(in_element == i, float(WEIGHTS[i]), weight_a)
    loads[6].wait()
    for f in range(FIELDS):
        loads[3 + f].wait()
    loads[7].wait()
    for which in range(2):
        high = lane_ops[which].astype(jnp.bfloat16)
        low = (lane_ops[which] - high.astype(jnp.float32)).astype(jnp.bfloat16)
        wts[which, :LANES, :LANES] = high
        wts[which, :LANES, LANES:] = low
        wts[which, LANES:, :LANES] = high
        wts[which, LANES:, LANES:] = jnp.zeros((LANES, LANES), jnp.bfloat16)
    for z in range(8):
        for i in range(8):
            weight = float(WEIGHTS[z] * WEIGHTS[i]) * weight_a
            massive[z * 8 + i] = weight * mas[z, pl.ds(i, 8, stride=8), :]
            for f in range(FIELDS):
                scaled[f, z * 8 + i] = weight * native(dif, f, z, i)

    for f in range(FIELDS):

        def keep_rhs(z, i, tile, total):
            full[0, f, z * 8 + i] = tile
            rhs_out[f, z, pl.ds(i, 8, stride=8), :] = tile
            return total + tile * native(src, f, z, i)

        dots[f] = complete(0, f, keep_rhs, zeros)
        dots[3 + f] = operate(0, f)
        send(1, f)

    for f in range(FIELDS):

        def keep_image(z, i, tile, total):
            full[1, f, z * 8 + i] = tile
            image_out[f, z, pl.ds(i, 8, stride=8), :] = tile
            return total + tile * raw[f, z * 8 + i]

        dots[6 + f] = complete(1, f, keep_image, zeros)
        dots[9 + f] = operate(1, f)
        send(2, f)

    lane_row = lax.broadcasted_iota(jnp.int32, (1, LANES), 1)
    row = jnp.zeros((1, LANES), jnp.float32)
    for j in range(12):
        part = jnp.sum(jnp.sum(dots[j], axis=0, keepdims=True), axis=1, keepdims=True)
        row = jnp.where(lane_row == j, part, row)

    def exchange(stage, partners, row):
        ar_send[stage] = row
        sent = []
        for j, device in enumerate(partners):
            copy = pltpu.make_async_remote_copy(
                src_ref=ar_send.at[stage],
                dst_ref=ar_got.at[stage, j],
                send_sem=ar_send_sem.at[stage, j],
                recv_sem=ar_recv_sem.at[stage, j],
                device_id=device,
                device_id_type=MESH,
            )
            copy.start()
            sent.append(copy)
        return sent

    def gathered(stage, sent, row):
        for copy in sent:
            copy.wait_recv()
        return row + jnp.sum(ar_got[stage], axis=0)

    first = exchange(0, column, row)
    row = gathered(0, first, row)
    second = exchange(1, plane, row)

    for f in range(FIELDS):

        def keep_second(z, i, tile, carry):
            twice_out[f, z, pl.ds(i, 8, stride=8), :] = tile
            return carry

        complete(2, f, keep_second, 0)

    row = gathered(1, second, row)

    def moved(count):
        return pltpu.roll(jnp.broadcast_to(row, (8, LANES)), LANES - count, 1)

    norm = jnp.where(lane < FIELDS, jnp.broadcast_to(row, (8, LANES)), 1.0)
    beta = moved(3) / norm
    gamma = moved(6) / norm
    delta = moved(9) / norm
    below = beta * delta - gamma * gamma
    below = jnp.where(lane < FIELDS, below, 1.0)
    one_image = (delta - beta * gamma) / below
    two_images = (gamma - beta * beta) / below

    coef_out[0] = one_image
    coef_out[1] = two_images

    for copy in first + second:
        copy.wait_send()
    for ph in range(PHASES):
        for f in range(FIELDS):
            finish_sends(ph, f)


def combine(rhs, image, twice, coefs, sol_hbm, res_hbm, sol, res, sems):
    rows = 8 // PIECES
    copies = []
    for f in range(FIELDS):
        c = jnp.broadcast_to(coefs[0][:, f : f + 1], (8, LANES))
        d = jnp.broadcast_to(coefs[1][:, f : f + 1], (8, LANES))
        for piece in range(PIECES):
            part = pl.ds(piece * rows, rows)
            for z in range(piece * rows, (piece + 1) * rows):
                for e in range(8):
                    at = (f, z, pl.ds(e * 8, 8))
                    first = image[at]
                    sol[at] = c * rhs[at] - d * first
                    res[at] = rhs[at] - c * first + d * twice[at]
            for k, (vmem, hbm) in enumerate(((sol, sol_hbm), (res, res_hbm))):
                copy = pltpu.make_async_copy(
                    vmem.at[f, part], hbm.at[f, part], sems.at[k, f, piece]
                )
                copy.start()
                copies.append(copy)
    for copy in copies:
        copy.wait()


def shards(source_terms, diffusion, mass_coefficient):
    shape = source_terms.shape
    field = (FIELDS, TILES, 8, LANES)
    f32 = jnp.float32
    operators = jnp.asarray(lane_operators())
    rhs, image, twice, coefs = pl.pallas_call(
        kernel,
        out_shape=tuple(
            jax.ShapeDtypeStruct(s, f32) for s in (shape, shape, shape, (2, 8, LANES))
        ),
        in_specs=[pl.BlockSpec(memory_space=pltpu.HBM)] * 4,
        out_specs=(pl.BlockSpec(memory_space=pltpu.VMEM),) * 4,
        scratch_shapes=[
            pltpu.VMEM(shape, f32),
            pltpu.VMEM(shape, f32),
            pltpu.VMEM(mass_coefficient.shape, f32),
            pltpu.VMEM((2, LANES, LANES), f32),
            pltpu.VMEM((2, 2 * LANES, 2 * LANES), jnp.bfloat16),
            pltpu.VMEM(field, f32),
            pltpu.VMEM(field[1:], f32),
            pltpu.VMEM((PHASES,) + field, f32),
            pltpu.VMEM((2,) + field, f32),
            pltpu.VMEM(field, f32),
            pltpu.VMEM((PHASES, FIELDS, 8, LANES), f32),
            pltpu.VMEM((PHASES, FIELDS, 2, 8, 8, LANES), f32),
            pltpu.VMEM((PHASES, FIELDS, 6, 8, LANES), f32),
            pltpu.VMEM((12, 8, LANES), f32),
            pltpu.VMEM((2, 1, LANES), f32),
            pltpu.VMEM((2, 15, 1, LANES), f32),
            pltpu.SemaphoreType.DMA((8,)),
            pltpu.SemaphoreType.DMA((PHASES, FIELDS, 8)),
            pltpu.SemaphoreType.DMA((PHASES, FIELDS, 8)),
            pltpu.SemaphoreType.DMA((2, 15)),
            pltpu.SemaphoreType.DMA((2, 15)),
        ],
        compiler_params=pltpu.CompilerParams(
            collective_id=0, has_side_effects=True, vmem_limit_bytes=40 * 1024 * 1024
        ),
    )(*(pltpu.with_memory_space_constraint(x, pltpu.HBM) for x in (source_terms, diffusion, mass_coefficient, operators)))
    return pl.pallas_call(
        combine,
        out_shape=(jax.ShapeDtypeStruct(shape, f32),) * 2,
        in_specs=[pl.BlockSpec(memory_space=pltpu.VMEM)] * 4,
        out_specs=(pl.BlockSpec(memory_space=pltpu.HBM),) * 2,
        scratch_shapes=[
            pltpu.VMEM(shape, f32),
            pltpu.VMEM(shape, f32),
            pltpu.SemaphoreType.DMA((2, FIELDS, PIECES)),
        ],
    )(*(pltpu.with_memory_space_constraint(x, pltpu.VMEM) for x in (rhs, image, twice, coefs)))


def solution(mesh):
    in_specs = (
        P(None, "axial", None, "azi"),
        P(None, "axial", None, "azi"),
        P("axial", None, "azi"),
    )
    out_specs = (P(None, "axial", None, "azi"), P(None, "axial", None, "azi"))
    return jax.shard_map(shards, mesh=mesh, in_specs=in_specs, out_specs=out_specs, check_vma=False)
```

```python
import jax
import jax.numpy as jnp
import numpy as np
from jax import lax
from jax.experimental import pallas as pl
from jax.experimental.pallas import tpu as pltpu
from jax.sharding import PartitionSpec as P

MESH = pl.DeviceIdType.MESH
FIELDS = 3
PHASES = 3
PIECES = 1
LANES = 128
TILES = 64


def gll_tables():
    degree = 7
    points = np.array(
        [
            -1.0,
            -0.8717401485096066,
            -0.5917001814331423,
            -0.2092992179024789,
            0.2092992179024789,
            0.5917001814331423,
            0.8717401485096066,
            1.0,
        ]
    )
    previous = np.ones(degree + 1)
    current = points.copy()
    for order in range(1, degree):
        following = ((2 * order + 1) * points * current - order * previous) / (order + 1)
        previous = current
        current = following
    weights = 2.0 / (degree * (degree + 1) * current * current)
    derivative = np.zeros((degree + 1, degree + 1))
    for first_index in range(degree + 1):
        for second_index in range(degree + 1):
            if first_index != second_index:
                derivative[first_index, second_index] = current[first_index] / (
                    current[second_index] * (points[first_index] - points[second_index])
                )
    derivative[0, 0] = -degree * (degree + 1) / 4.0
    derivative[degree, degree] = degree * (degree + 1) / 4.0
    return (weights, derivative)


WEIGHTS, DERIVATIVE = gll_tables()


def lane_operators():
    whole = np.kron(np.eye(LANES // 8), DERIVATIVE)
    return np.stack([whole.T, whole]).astype(np.float32)


def mix(matrix, values):
    even = [values[i] + values[7 - i] for i in range(4)]
    odd = [values[i] - values[7 - i] for i in range(4)]
    result = [None] * 8
    for j in range(4):
        from_even = None
        from_odd = None
        for i in range(4):
            a = float(0.5 * (matrix[j, i] + matrix[j, 7 - i])) * even[i]
            b = float(0.5 * (matrix[j, i] - matrix[j, 7 - i])) * odd[i]
            from_even = a if from_even is None else from_even + a
            from_odd = b if from_odd is None else from_odd + b
        result[j] = from_odd + from_even
        result[7 - j] = from_odd - from_even
    return result


def azi_shift(azi, axial, count):
    return lax.rem(azi + count + 64, 64), axial


def column_partner(azi, axial, index):
    z = lax.rem(azi, 8)
    other = azi - z + lax.rem(z + index // 2, 8)
    core = lax.rem(axial, 2)
    flipped = axial + (1 - 2 * core) if index % 2 else axial
    return other, flipped


def plane_partner(azi, axial, index):
    x = azi // 16
    y_hi = lax.rem(azi // 8, 2)
    z = lax.rem(azi, 8)
    x = lax.rem(x + index // 4, 4)
    y_hi = lax.rem(y_hi + (index // 2) % 2, 2)
    return x * 16 + y_hi * 8 + z, lax.rem(axial + 2 * (index % 2), 4)


def kernel(
    src_hbm,
    dif_hbm,
    mas_hbm,
    wts_hbm,
    rhs_out,
    image_out,
    twice_out,
    coef_out,
    src,
    dif,
    mas,
    lane_ops,
    wts,
    scaled,
    massive,
    own,
    full,
    raw,
    packed,
    got_plane,
    got_packed,
    dots,
    ar_send,
    ar_got,
    in_sem,
    send_sem,
    recv_sem,
    ar_send_sem,
    ar_recv_sem,
):
    azi = lax.axis_index("azi")
    axial = lax.axis_index("axial")
    has_low = axial > 0
    has_high = axial < 3

    loads = []
    for f in range(FIELDS):
        loads.append(pltpu.make_async_copy(src_hbm.at[f], src.at[f], in_sem.at[f]))
    for f in range(FIELDS):
        loads.append(pltpu.make_async_copy(dif_hbm.at[f], dif.at[f], in_sem.at[3 + f]))
    loads.append(pltpu.make_async_copy(mas_hbm, mas, in_sem.at[6]))
    loads.append(pltpu.make_async_copy(wts_hbm, lane_ops, in_sem.at[7]))
    for copy in loads:
        copy.start()

    up = lax.rem(azi + 1, 64)
    down = lax.rem(azi + 63, 64)
    barrier = pltpu.get_barrier_semaphore()

    def greet(device):
        pl.semaphore_signal(barrier, inc=1, device_id=device, device_id_type=MESH)

    greet((up, axial))
    greet((down, axial))

    @pl.when(has_low)
    def _():
        for other in (up, azi, down):
            greet((other, axial - 1))

    @pl.when(has_high)
    def _():
        for other in (up, azi, down):
            greet((other, axial + 1))

    column = [column_partner(azi, axial, j) for j in range(1, 16)]
    plane = [plane_partner(azi, axial, j) for j in range(1, 16)]
    for device in column + plane:
        greet(device)

    @pl.when(jnp.logical_not(has_low))
    def _():
        for ph in range(PHASES):
            for f in range(FIELDS):
                got_plane[ph, f, 0] = jnp.zeros((8, 8, LANES), jnp.float32)
                got_packed[ph, f, 2] = jnp.zeros((8, LANES), jnp.float32)
                got_packed[ph, f, 3] = jnp.zeros((8, LANES), jnp.float32)

    @pl.when(jnp.logical_not(has_high))
    def _():
        for ph in range(PHASES):
            for f in range(FIELDS):
                got_plane[ph, f, 1] = jnp.zeros((8, 8, LANES), jnp.float32)
                got_packed[ph, f, 4] = jnp.zeros((8, LANES), jnp.float32)
                got_packed[ph, f, 5] = jnp.zeros((8, LANES), jnp.float32)

    lane = lax.broadcasted_iota(jnp.int32, (8, LANES), 1)
    sub = lax.broadcasted_iota(jnp.int32, (8, LANES), 0)
    in_element = lane % 8
    starts = (in_element == 0) & (lane != 0)
    finish = (in_element == 7) & (lane != LANES - 1)
    outer = (lane == 0) | (lane == LANES - 1)
    even_lane = lane % 2 == 0
    group_of_lane = ((lane + 1) % LANES) // 16
    pair_of_lane = ((lane + 1) % LANES) // 2
    zeros = jnp.zeros((8, LANES), jnp.float32)

    def join_lanes(tile):
        before = pltpu.roll(tile, 1, 1)
        after = pltpu.roll(tile, LANES - 1, 1)
        return tile + jnp.where(starts, before, jnp.where(finish, after, 0.0))

    def join_rows(tiles):
        first, last = tiles[0], tiles[7]
        tiles[0] = first + jnp.where(sub > 0, pltpu.roll(last, 1, 0), 0.0)
        tiles[7] = last + jnp.where(sub < 7, pltpu.roll(first, 7, 0), 0.0)
        return tiles

    def assemble_own(ph, f, z, tiles, faces):
        tiles = join_rows(list(tiles))
        line = zeros
        for i in range(8):
            tile = join_lanes(tiles[i])
            own[ph, f, z * 8 + i] = tile
            turned = pltpu.roll(tile, 2 * i, 1) if i else tile
            line = jnp.where(pair_of_lane == i, turned, line)
        return jnp.where(group_of_lane == z, pltpu.roll(line, z * 16, 1) if z else line, faces)

    def copies(ph, f):
        def remote(source, target, slot, device):
            return pltpu.make_async_remote_copy(
                src_ref=source,
                dst_ref=target,
                send_sem=send_sem.at[ph, f, slot],
                recv_sem=recv_sem.at[ph, f, slot],
                device_id=device,
                device_id_type=MESH,
            )

        tile = packed.at[ph, f]
        slots = got_packed.at[ph, f]
        always = [
            remote(tile, slots.at[0], 0, (up, axial)),
            remote(tile, slots.at[1], 1, (down, axial)),
        ]
        above = [
            remote(tile, slots.at[2], 2, (up, axial + 1)),
            remote(tile, slots.at[3], 3, (down, axial + 1)),
            remote(own.at[ph, f, pl.ds(56, 8)], got_plane.at[ph, f, 0], 6, (azi, axial + 1)),
        ]
        below = [
            remote(tile, slots.at[4], 4, (up, axial - 1)),
            remote(tile, slots.at[5], 5, (down, axial - 1)),
            remote(own.at[ph, f, pl.ds(0, 8)], got_plane.at[ph, f, 1], 7, (azi, axial - 1)),
        ]
        return always, above, below

    def send(ph, f):
        always, above, below = copies(ph, f)
        for copy in always:
            copy.start()

        @pl.when(has_high)
        def _():
            for copy in above:
                copy.start()

        @pl.when(has_low)
        def _():
            for copy in below:
                copy.start()

    def receive(ph, f):
        always, above, below = copies(ph, f)
        for copy in always:
            copy.wait_recv()

        @pl.when(has_low)
        def _():
            for copy in above:
                copy.wait_recv()

        @pl.when(has_high)
        def _():
            for copy in below:
                copy.wait_recv()

    def finish_sends(ph, f):
        always, above, below = copies(ph, f)
        for copy in always:
            copy.wait_send()

        @pl.when(has_high)
        def _():
            for copy in above:
                copy.wait_send()

        @pl.when(has_low)
        def _():
            for copy in below:
                copy.wait_send()

    def complete(ph, f, use, carry):
        receive(ph, f)

        def faced(left, right):
            return jnp.where(
                even_lane, pltpu.roll(left, 1, 1), pltpu.roll(right, LANES - 1, 1)
            )

        slots = [got_packed[ph, f, s] for s in range(6)]
        faces = faced(slots[0], slots[1])
        low = pltpu.roll(faced(slots[2], slots[3]), LANES - 112, 1)
        high = pltpu.roll(faced(slots[4], slots[5]), 112, 1)
        faces = faces + jnp.where(group_of_lane == 0, low, 0.0)
        faces = faces + jnp.where(group_of_lane == 7, high, 0.0)

        def one(z, carry, plane):
            line = pltpu.roll(faces, LANES - z * 16, 1) if z else faces
            for i in range(8):
                turned = pltpu.roll(line, LANES - 2 * i, 1) if i else line
                tile = own[ph, f, z * 8 + i] + jnp.where(outer, turned, 0.0)
                if plane is not None:
                    tile = tile + got_plane[ph, f, plane, i]
                carry = use(z, i, tile, carry)
            return carry

        carry = one(0, carry, 0)
        for z in range(1, 7):
            carry = one(z, carry, None)
        return one(7, carry, 1)

    def split_dot(values, which):
        high = values.astype(jnp.bfloat16)
        low = (values - high.astype(jnp.float32)).astype(jnp.bfloat16)
        both = jnp.dot(
            jnp.concatenate([high, low], axis=1), wts[which], preferred_element_type=jnp.float32
        )
        return both[:, :LANES] + both[:, LANES:]

    def operate(k, f):
        values = full[k, f].reshape(TILES * 8, LANES)
        gradient = split_dot(values, 0) * scaled[f].reshape(TILES * 8, LANES)
        raw[f] = split_dot(gradient, 1).reshape(TILES, 8, LANES)

        def along_axial(i, carry):
            tiles = [full[k, f, z * 8 + i] for z in range(8)]
            gradient = mix(DERIVATIVE, tiles)
            gradient = [scaled[f, z * 8 + i] * gradient[z] for z in range(8)]
            back = mix(DERIVATIVE.T, gradient)
            for z in range(8):
                raw[f, z * 8 + i] = raw[f, z * 8 + i] + (back[z] + massive[z * 8 + i] * tiles[z])
            return carry

        for i in range(8):
            along_axial(i, 0)

        def along_radius(z, carry):
            total, faces = carry
            tiles = [full[k, f, z * 8 + i] for i in range(8)]
            gradient = mix(DERIVATIVE, tiles)
            gradient = [scaled[f, z * 8 + i] * gradient[i] for i in range(8)]
            back = mix(DERIVATIVE.T, gradient)
            back = [raw[f, z * 8 + i] + back[i] for i in range(8)]
            for i in range(8):
                total = total + tiles[i] * back[i]
                raw[f, z * 8 + i] = back[i]
            return total, assemble_own(k + 1, f, z, back, faces)

        total, faces = zeros, zeros
        for z in range(8):
            total, faces = along_radius(z, (total, faces))
        packed[k + 1, f] = faces
        return total

    def native(ref, f, z, i):
        return ref[f, z, pl.ds(i, 8, stride=8), :]

    for f in range(FIELDS):
        loads[f].wait()

        def gather(z, faces):
            return assemble_own(0, f, z, [native(src, f, z, i) for i in range(8)], faces)

        faces = zeros
        for z in range(8):
            faces = gather(z, faces)
        packed[0, f] = faces

    around = axial * 0 + 2 + 30 + jnp.where(has_low, 3, 0) + jnp.where(has_high, 3, 0)
    pl.semaphore_wait(barrier, around)
    for f in range(FIELDS):
        send(0, f)

    weight_a = jnp.zeros((8, LANES), jnp.float32)
    for i in range(8):
        weight_a = jnp.where(in_element == i, float(WEIGHTS[i]), weight_a)
    loads[6].wait()
    for f in range(FIELDS):
        loads[3 + f].wait()
    loads[7].wait()
    for which in range(2):
        high = lane_ops[which].astype(jnp.bfloat16)
        low = (lane_ops[which] - high.astype(jnp.float32)).astype(jnp.bfloat16)
        wts[which, :LANES, :LANES] = high
        wts[which, :LANES, LANES:] = low
        wts[which, LANES:, :LANES] = high
        wts[which, LANES:, LANES:] = jnp.zeros((LANES, LANES), jnp.bfloat16)
    for z in range(8):
        for i in range(8):
            weight = float(WEIGHTS[z] * WEIGHTS[i]) * weight_a
            massive[z * 8 + i] = weight * mas[z, pl.ds(i, 8, stride=8), :]
            for f in range(FIELDS):
                scaled[f, z * 8 + i] = weight * native(dif, f, z, i)

    for f in range(FIELDS):

        def keep_rhs(z, i, tile, total):
            full[0, f, z * 8 + i] = tile
            return total + tile * native(src, f, z, i)

        dots[f] = complete(0, f, keep_rhs, zeros)
        dots[3 + f] = operate(0, f)
        send(1, f)

    for f in range(FIELDS):

        def keep_image(z, i, tile, total):
            full[1, f, z * 8 + i] = tile
            return total + tile * raw[f, z * 8 + i]

        dots[6 + f] = complete(1, f, keep_image, zeros)
        dots[9 + f] = operate(1, f)
        send(2, f)

    lane_row = lax.broadcasted_iota(jnp.int32, (1, LANES), 1)
    row = jnp.zeros((1, LANES), jnp.float32)
    for j in range(12):
        part = jnp.sum(jnp.sum(dots[j], axis=0, keepdims=True), axis=1, keepdims=True)
        row = jnp.where(lane_row == j, part, row)

    def exchange(stage, partners, row):
        ar_send[stage] = row
        sent = []
        for j, device in enumerate(partners):
            copy = pltpu.make_async_remote_copy(
                src_ref=ar_send.at[stage],
                dst_ref=ar_got.at[stage, j],
                send_sem=ar_send_sem.at[stage, j],
                recv_sem=ar_recv_sem.at[stage, j],
                device_id=device,
                device_id_type=MESH,
            )
            copy.start()
            sent.append(copy)
        return sent

    def gathered(stage, sent, row):
        for copy in sent:
            copy.wait_recv()
        return row + jnp.sum(ar_got[stage], axis=0)

    first = exchange(0, column, row)
    row = gathered(0, first, row)
    second = exchange(1, plane, row)
    for f in range(FIELDS):
        for z in range(8):
            for i in range(8):
                rhs_out[f, z, pl.ds(i, 8, stride=8), :] = full[0, f, z * 8 + i]
                image_out[f, z, pl.ds(i, 8, stride=8), :] = full[1, f, z * 8 + i]

    for f in range(FIELDS):

        def keep_second(z, i, tile, carry):
            twice_out[f, z, pl.ds(i, 8, stride=8), :] = tile
            return carry

        complete(2, f, keep_second, 0)

    for copy in first + second:
        copy.wait_send()
    for ph in range(PHASES):
        for f in range(FIELDS):
            finish_sends(ph, f)
    row = gathered(1, second, row)

    def moved(count):
        return pltpu.roll(jnp.broadcast_to(row, (8, LANES)), LANES - count, 1)

    norm = jnp.where(lane < FIELDS, jnp.broadcast_to(row, (8, LANES)), 1.0)
    beta = moved(3) / norm
    gamma = moved(6) / norm
    delta = moved(9) / norm
    below = beta * delta - gamma * gamma
    below = jnp.where(lane < FIELDS, below, 1.0)
    one_image = (delta - beta * gamma) / below
    two_images = (gamma - beta * beta) / below

    coef_out[0] = one_image
    coef_out[1] = two_images


def combine(rhs, image, twice, coefs, sol_hbm, res_hbm, sol, res, sems):
    rows = 8 // PIECES
    copies = []
    for f in range(FIELDS):
        c = jnp.broadcast_to(coefs[0][:, f : f + 1], (8, LANES))
        d = jnp.broadcast_to(coefs[1][:, f : f + 1], (8, LANES))
        for piece in range(PIECES):
            part = pl.ds(piece * rows, rows)
            for z in range(piece * rows, (piece + 1) * rows):
                for e in range(8):
                    at = (f, z, pl.ds(e * 8, 8))
                    first = image[at]
                    sol[at] = c * rhs[at] - d * first
                    res[at] = rhs[at] - c * first + d * twice[at]
            for k, (vmem, hbm) in enumerate(((sol, sol_hbm), (res, res_hbm))):
                copy = pltpu.make_async_copy(
                    vmem.at[f, part], hbm.at[f, part], sems.at[k, f, piece]
                )
                copy.start()
                copies.append(copy)
    for copy in copies:
        copy.wait()


def shards(source_terms, diffusion, mass_coefficient):
    shape = source_terms.shape
    field = (FIELDS, TILES, 8, LANES)
    f32 = jnp.float32
    operators = jnp.asarray(lane_operators())
    rhs, image, twice, coefs = pl.pallas_call(
        kernel,
        out_shape=tuple(
            jax.ShapeDtypeStruct(s, f32) for s in (shape, shape, shape, (2, 8, LANES))
        ),
        in_specs=[pl.BlockSpec(memory_space=pltpu.HBM)] * 4,
        out_specs=(pl.BlockSpec(memory_space=pltpu.VMEM),) * 4,
        scratch_shapes=[
            pltpu.VMEM(shape, f32),
            pltpu.VMEM(shape, f32),
            pltpu.VMEM(mass_coefficient.shape, f32),
            pltpu.VMEM((2, LANES, LANES), f32),
            pltpu.VMEM((2, 2 * LANES, 2 * LANES), jnp.bfloat16),
            pltpu.VMEM(field, f32),
            pltpu.VMEM(field[1:], f32),
            pltpu.VMEM((PHASES,) + field, f32),
            pltpu.VMEM((2,) + field, f32),
            pltpu.VMEM(field, f32),
            pltpu.VMEM((PHASES, FIELDS, 8, LANES), f32),
            pltpu.VMEM((PHASES, FIELDS, 2, 8, 8, LANES), f32),
            pltpu.VMEM((PHASES, FIELDS, 6, 8, LANES), f32),
            pltpu.VMEM((12, 8, LANES), f32),
            pltpu.VMEM((2, 1, LANES), f32),
            pltpu.VMEM((2, 15, 1, LANES), f32),
            pltpu.SemaphoreType.DMA((8,)),
            pltpu.SemaphoreType.DMA((PHASES, FIELDS, 8)),
            pltpu.SemaphoreType.DMA((PHASES, FIELDS, 8)),
            pltpu.SemaphoreType.DMA((2, 15)),
            pltpu.SemaphoreType.DMA((2, 15)),
        ],
        compiler_params=pltpu.CompilerParams(
            collective_id=0, has_side_effects=True, vmem_limit_bytes=40 * 1024 * 1024
        ),
    )(*(pltpu.with_memory_space_constraint(x, pltpu.HBM) for x in (source_terms, diffusion, mass_coefficient, operators)))
    return pl.pallas_call(
        combine,
        out_shape=(jax.ShapeDtypeStruct(shape, f32),) * 2,
        in_specs=[pl.BlockSpec(memory_space=pltpu.VMEM)] * 4,
        out_specs=(pl.BlockSpec(memory_space=pltpu.HBM),) * 2,
        scratch_shapes=[
            pltpu.VMEM(shape, f32),
            pltpu.VMEM(shape, f32),
            pltpu.SemaphoreType.DMA((2, FIELDS, PIECES)),
        ],
    )(*(pltpu.with_memory_space_constraint(x, pltpu.VMEM) for x in (rhs, image, twice, coefs)))


def solution(mesh):
    in_specs = (
        P(None, "axial", None, "azi"),
        P(None, "axial", None, "azi"),
        P("axial", None, "azi"),
    )
    out_specs = (P(None, "axial", None, "azi"), P(None, "axial", None, "azi"))
    return jax.shard_map(shards, mesh=mesh, in_specs=in_specs, out_specs=out_specs, check_vma=False)
```

```python
import jax
import jax.numpy as jnp
import numpy as np
from jax import lax
from jax.experimental import pallas as pl
from jax.experimental.pallas import tpu as pltpu
from jax.sharding import PartitionSpec as P

MESH = pl.DeviceIdType.MESH
FIELDS = 3
PHASES = 3
PIECES = 1
LANES = 128
TILES = 64


def gll_tables():
    degree = 7
    points = np.array(
        [
            -1.0,
            -0.8717401485096066,
            -0.5917001814331423,
            -0.2092992179024789,
            0.2092992179024789,
            0.5917001814331423,
            0.8717401485096066,
            1.0,
        ]
    )
    previous = np.ones(degree + 1)
    current = points.copy()
    for order in range(1, degree):
        following = ((2 * order + 1) * points * current - order * previous) / (order + 1)
        previous = current
        current = following
    weights = 2.0 / (degree * (degree + 1) * current * current)
    derivative = np.zeros((degree + 1, degree + 1))
    for first_index in range(degree + 1):
        for second_index in range(degree + 1):
            if first_index != second_index:
                derivative[first_index, second_index] = current[first_index] / (
                    current[second_index] * (points[first_index] - points[second_index])
                )
    derivative[0, 0] = -degree * (degree + 1) / 4.0
    derivative[degree, degree] = degree * (degree + 1) / 4.0
    return (weights, derivative)


WEIGHTS, DERIVATIVE = gll_tables()


def lane_operators():
    whole = np.kron(np.eye(LANES // 8), DERIVATIVE)
    return np.stack([whole.T, whole]).astype(np.float32)


def mix(matrix, values):
    even = [values[i] + values[7 - i] for i in range(4)]
    odd = [values[i] - values[7 - i] for i in range(4)]
    result = [None] * 8
    for j in range(4):
        from_even = None
        from_odd = None
        for i in range(4):
            a = float(0.5 * (matrix[j, i] + matrix[j, 7 - i])) * even[i]
            b = float(0.5 * (matrix[j, i] - matrix[j, 7 - i])) * odd[i]
            from_even = a if from_even is None else from_even + a
            from_odd = b if from_odd is None else from_odd + b
        result[j] = from_odd + from_even
        result[7 - j] = from_odd - from_even
    return result


def azi_shift(azi, axial, count):
    return lax.rem(azi + count + 64, 64), axial


def column_partner(azi, axial, index):
    z = lax.rem(azi, 8)
    other = azi - z + lax.rem(z + index // 2, 8)
    core = lax.rem(axial, 2)
    flipped = axial + (1 - 2 * core) if index % 2 else axial
    return other, flipped


def plane_partner(azi, axial, index):
    x = azi // 16
    y_hi = lax.rem(azi // 8, 2)
    z = lax.rem(azi, 8)
    x = lax.rem(x + index // 4, 4)
    y_hi = lax.rem(y_hi + (index // 2) % 2, 2)
    return x * 16 + y_hi * 8 + z, lax.rem(axial + 2 * (index % 2), 4)


def kernel(
    src_hbm,
    dif_hbm,
    mas_hbm,
    wts_hbm,
    rhs_out,
    image_out,
    twice_out,
    coef_out,
    src,
    dif,
    mas,
    lane_ops,
    wts,
    scaled,
    massive,
    own,
    full,
    raw,
    packed,
    got_plane,
    got_packed,
    dots,
    ar_send,
    ar_got,
    in_sem,
    send_sem,
    recv_sem,
    ar_send_sem,
    ar_recv_sem,
):
    azi = lax.axis_index("azi")
    axial = lax.axis_index("axial")
    has_low = axial > 0
    has_high = axial < 3

    loads = []
    for f in range(FIELDS):
        loads.append(pltpu.make_async_copy(src_hbm.at[f], src.at[f], in_sem.at[f]))
    for f in range(FIELDS):
        loads.append(pltpu.make_async_copy(dif_hbm.at[f], dif.at[f], in_sem.at[3 + f]))
    loads.append(pltpu.make_async_copy(mas_hbm, mas, in_sem.at[6]))
    loads.append(pltpu.make_async_copy(wts_hbm, lane_ops, in_sem.at[7]))
    for copy in loads:
        copy.start()

    up = lax.rem(azi + 1, 64)
    down = lax.rem(azi + 63, 64)
    barrier = pltpu.get_barrier_semaphore()

    def greet(device):
        pl.semaphore_signal(barrier, inc=1, device_id=device, device_id_type=MESH)

    greet((up, axial))
    greet((down, axial))

    @pl.when(has_low)
    def _():
        for other in (up, azi, down):
            greet((other, axial - 1))

    @pl.when(has_high)
    def _():
        for other in (up, azi, down):
            greet((other, axial + 1))

    column = [column_partner(azi, axial, j) for j in range(1, 16)]
    plane = [plane_partner(azi, axial, j) for j in range(1, 16)]
    for device in column + plane:
        greet(device)

    @pl.when(jnp.logical_not(has_low))
    def _():
        for ph in range(PHASES):
            for f in range(FIELDS):
                got_plane[ph, f, 0] = jnp.zeros((8, 8, LANES), jnp.float32)
                got_packed[ph, f, 2] = jnp.zeros((8, LANES), jnp.float32)
                got_packed[ph, f, 3] = jnp.zeros((8, LANES), jnp.float32)

    @pl.when(jnp.logical_not(has_high))
    def _():
        for ph in range(PHASES):
            for f in range(FIELDS):
                got_plane[ph, f, 1] = jnp.zeros((8, 8, LANES), jnp.float32)
                got_packed[ph, f, 4] = jnp.zeros((8, LANES), jnp.float32)
                got_packed[ph, f, 5] = jnp.zeros((8, LANES), jnp.float32)

    lane = lax.broadcasted_iota(jnp.int32, (8, LANES), 1)
    sub = lax.broadcasted_iota(jnp.int32, (8, LANES), 0)
    in_element = lane % 8
    starts = (in_element == 0) & (lane != 0)
    finish = (in_element == 7) & (lane != LANES - 1)
    outer = (lane == 0) | (lane == LANES - 1)
    even_lane = lane % 2 == 0
    group_of_lane = ((lane + 1) % LANES) // 16
    pair_of_lane = ((lane + 1) % LANES) // 2
    zeros = jnp.zeros((8, LANES), jnp.float32)

    def join_lanes(tile):
        before = pltpu.roll(tile, 1, 1)
        after = pltpu.roll(tile, LANES - 1, 1)
        return tile + jnp.where(starts, before, jnp.where(finish, after, 0.0))

    def join_rows(tiles):
        first, last = tiles[0], tiles[7]
        tiles[0] = first + jnp.where(sub > 0, pltpu.roll(last, 1, 0), 0.0)
        tiles[7] = last + jnp.where(sub < 7, pltpu.roll(first, 7, 0), 0.0)
        return tiles

    def assemble_own(ph, f, z, tiles, faces):
        tiles = join_rows(list(tiles))
        line = zeros
        for i in range(8):
            tile = join_lanes(tiles[i])
            own[ph, f, z * 8 + i] = tile
            turned = pltpu.roll(tile, 2 * i, 1) if i else tile
            line = jnp.where(pair_of_lane == i, turned, line)
        return jnp.where(group_of_lane == z, pltpu.roll(line, z * 16, 1) if z else line, faces)

    def copies(ph, f):
        def remote(source, target, slot, device):
            return pltpu.make_async_remote_copy(
                src_ref=source,
                dst_ref=target,
                send_sem=send_sem.at[ph, f, slot],
                recv_sem=recv_sem.at[ph, f, slot],
                device_id=device,
                device_id_type=MESH,
            )

        tile = packed.at[ph, f]
        slots = got_packed.at[ph, f]
        always = [
            remote(tile, slots.at[0], 0, (up, axial)),
            remote(tile, slots.at[1], 1, (down, axial)),
        ]
        above = [
            remote(tile, slots.at[2], 2, (up, axial + 1)),
            remote(tile, slots.at[3], 3, (down, axial + 1)),
            remote(own.at[ph, f, pl.ds(56, 8)], got_plane.at[ph, f, 0], 6, (azi, axial + 1)),
        ]
        below = [
            remote(tile, slots.at[4], 4, (up, axial - 1)),
            remote(tile, slots.at[5], 5, (down, axial - 1)),
            remote(own.at[ph, f, pl.ds(0, 8)], got_plane.at[ph, f, 1], 7, (azi, axial - 1)),
        ]
        return always, above, below

    def send(ph, f):
        always, above, below = copies(ph, f)
        for copy in always:
            copy.start()

        @pl.when(has_high)
        def _():
            for copy in above:
                copy.start()

        @pl.when(has_low)
        def _():
            for copy in below:
                copy.start()

    def receive(ph, f):
        always, above, below = copies(ph, f)
        for copy in always:
            copy.wait_recv()

        @pl.when(has_low)
        def _():
            for copy in above:
                copy.wait_recv()

        @pl.when(has_high)
        def _():
            for copy in below:
                copy.wait_recv()

    def finish_sends(ph, f):
        always, above, below = copies(ph, f)
        for copy in always:
            copy.wait_send()

        @pl.when(has_high)
        def _():
            for copy in above:
                copy.wait_send()

        @pl.when(has_low)
        def _():
            for copy in below:
                copy.wait_send()

    def complete(ph, f, use, carry):
        receive(ph, f)

        def faced(left, right):
            return jnp.where(
                even_lane, pltpu.roll(left, 1, 1), pltpu.roll(right, LANES - 1, 1)
            )

        slots = [got_packed[ph, f, s] for s in range(6)]
        faces = faced(slots[0], slots[1])
        low = pltpu.roll(faced(slots[2], slots[3]), LANES - 112, 1)
        high = pltpu.roll(faced(slots[4], slots[5]), 112, 1)
        faces = faces + jnp.where(group_of_lane == 0, low, 0.0)
        faces = faces + jnp.where(group_of_lane == 7, high, 0.0)

        def one(z, carry, plane):
            line = pltpu.roll(faces, LANES - z * 16, 1) if z else faces
            for i in range(8):
                turned = pltpu.roll(line, LANES - 2 * i, 1) if i else line
                tile = own[ph, f, z * 8 + i] + jnp.where(outer, turned, 0.0)
                if plane is not None:
                    tile = tile + got_plane[ph, f, plane, i]
                carry = use(z, i, tile, carry)
            return carry

        carry = one(0, carry, 0)
        for z in range(1, 7):
            carry = one(z, carry, None)
        return one(7, carry, 1)

    def split_dot(values, which):
        high = values.astype(jnp.bfloat16)
        low = (values - high.astype(jnp.float32)).astype(jnp.bfloat16)
        both = jnp.dot(
            jnp.concatenate([high, low], axis=1), wts[which], preferred_element_type=jnp.float32
        )
        return both[:, :LANES] + both[:, LANES:]

    def operate(k, f):
        values = full[k, f].reshape(TILES * 8, LANES)
        gradient = split_dot(values, 0) * scaled[f].reshape(TILES * 8, LANES)
        raw[k, f] = split_dot(gradient, 1).reshape(TILES, 8, LANES)

        def along_axial(i, carry):
            tiles = [full[k, f, z * 8 + i] for z in range(8)]
            gradient = mix(DERIVATIVE, tiles)
            gradient = [scaled[f, z * 8 + i] * gradient[z] for z in range(8)]
            back = mix(DERIVATIVE.T, gradient)
            for z in range(8):
                raw[k, f, z * 8 + i] = raw[k, f, z * 8 + i] + (back[z] + massive[z * 8 + i] * tiles[z])
            return carry

        for i in range(8):
            along_axial(i, 0)

        def along_radius(z, carry):
            total, faces = carry
            tiles = [full[k, f, z * 8 + i] for i in range(8)]
            gradient = mix(DERIVATIVE, tiles)
            gradient = [scaled[f, z * 8 + i] * gradient[i] for i in range(8)]
            back = mix(DERIVATIVE.T, gradient)
            back = [raw[k, f, z * 8 + i] + back[i] for i in range(8)]
            for i in range(8):
                if k:
                    total = total + tiles[i] * back[i]
                else:
                    raw[k, f, z * 8 + i] = back[i]
            return total, assemble_own(k + 1, f, z, back, faces)

        total, faces = zeros, zeros
        for z in range(8):
            total, faces = along_radius(z, (total, faces))
        packed[k + 1, f] = faces
        return total

    def native(ref, f, z, i):
        return ref[f, z, pl.ds(i, 8, stride=8), :]

    for f in range(FIELDS):
        loads[f].wait()

        def gather(z, faces):
            return assemble_own(0, f, z, [native(src, f, z, i) for i in range(8)], faces)

        faces = zeros
        for z in range(8):
            faces = gather(z, faces)
        packed[0, f] = faces

    around = axial * 0 + 2 + 30 + jnp.where(has_low, 3, 0) + jnp.where(has_high, 3, 0)
    pl.semaphore_wait(barrier, around)
    for f in range(FIELDS):
        send(0, f)

    weight_a = jnp.zeros((8, LANES), jnp.float32)
    for i in range(8):
        weight_a = jnp.where(in_element == i, float(WEIGHTS[i]), weight_a)
    loads[6].wait()
    for f in range(FIELDS):
        loads[3 + f].wait()
    loads[7].wait()
    for which in range(2):
        high = lane_ops[which].astype(jnp.bfloat16)
        low = (lane_ops[which] - high.astype(jnp.float32)).astype(jnp.bfloat16)
        wts[which, :LANES, :LANES] = high
        wts[which, :LANES, LANES:] = low
        wts[which, LANES:, :LANES] = high
        wts[which, LANES:, LANES:] = jnp.zeros((LANES, LANES), jnp.bfloat16)
    for z in range(8):
        for i in range(8):
            weight = float(WEIGHTS[z] * WEIGHTS[i]) * weight_a
            massive[z * 8 + i] = weight * mas[z, pl.ds(i, 8, stride=8), :]
            for f in range(FIELDS):
                scaled[f, z * 8 + i] = weight * native(dif, f, z, i)

    for f in range(FIELDS):

        def keep_rhs(z, i, tile, total):
            full[0, f, z * 8 + i] = tile
            return total

        complete(0, f, keep_rhs, 0)
        operate(0, f)
        send(1, f)

    lane_row = lax.broadcasted_iota(jnp.int32, (1, LANES), 1)

    def add_to_row(row, j, total):
        part = jnp.sum(jnp.sum(total, axis=0, keepdims=True), axis=1, keepdims=True)
        return jnp.where(lane_row == j, part, row)

    row = jnp.zeros((1, LANES), jnp.float32)
    for f in range(FIELDS):
        alpha, beta = zeros, zeros
        for z in range(8):
            for i in range(8):
                tile = full[0, f, z * 8 + i]
                alpha = alpha + tile * native(src, f, z, i)
                beta = beta + tile * raw[0, f, z * 8 + i]
        row = add_to_row(row, f, alpha)
        row = add_to_row(row, 3 + f, beta)

    for f in range(FIELDS):

        def keep_image(z, i, tile, total):
            full[1, f, z * 8 + i] = tile
            return total + tile * raw[0, f, z * 8 + i]

        dots[6 + f] = complete(1, f, keep_image, zeros)
        dots[9 + f] = operate(1, f)
        send(2, f)

    for j in range(6, 12):
        row = add_to_row(row, j, dots[j])

    def exchange(stage, partners, row):
        ar_send[stage] = row
        sent = []
        for j, device in enumerate(partners):
            copy = pltpu.make_async_remote_copy(
                src_ref=ar_send.at[stage],
                dst_ref=ar_got.at[stage, j],
                send_sem=ar_send_sem.at[stage, j],
                recv_sem=ar_recv_sem.at[stage, j],
                device_id=device,
                device_id_type=MESH,
            )
            copy.start()
            sent.append(copy)
        return sent

    def gathered(stage, sent, row):
        for copy in sent:
            copy.wait_recv()
        return row + jnp.sum(ar_got[stage], axis=0)

    first = exchange(0, column, row)
    row = gathered(0, first, row)
    second = exchange(1, plane, row)
    for f in range(FIELDS):
        for z in range(8):
            for i in range(8):
                rhs_out[f, z, pl.ds(i, 8, stride=8), :] = full[0, f, z * 8 + i]
                image_out[f, z, pl.ds(i, 8, stride=8), :] = full[1, f, z * 8 + i]

    for f in range(FIELDS):

        def keep_second(z, i, tile, carry):
            twice_out[f, z, pl.ds(i, 8, stride=8), :] = tile
            return carry

        complete(2, f, keep_second, 0)

    for copy in first + second:
        copy.wait_send()
    for ph in range(PHASES):
        for f in range(FIELDS):
            finish_sends(ph, f)
    row = gathered(1, second, row)

    def moved(count):
        return pltpu.roll(jnp.broadcast_to(row, (8, LANES)), LANES - count, 1)

    norm = jnp.where(lane < FIELDS, jnp.broadcast_to(row, (8, LANES)), 1.0)
    beta = moved(3) / norm
    gamma = moved(6) / norm
    delta = moved(9) / norm
    below = beta * delta - gamma * gamma
    below = jnp.where(lane < FIELDS, below, 1.0)
    one_image = (delta - beta * gamma) / below
    two_images = (gamma - beta * beta) / below

    coef_out[0] = one_image
    coef_out[1] = two_images


def combine(rhs, image, twice, coefs, sol_hbm, res_hbm, sol, res, sems):
    rows = 8 // PIECES
    copies = []
    for f in range(FIELDS):
        c = jnp.broadcast_to(coefs[0][:, f : f + 1], (8, LANES))
        d = jnp.broadcast_to(coefs[1][:, f : f + 1], (8, LANES))
        for piece in range(PIECES):
            part = pl.ds(piece * rows, rows)
            for z in range(piece * rows, (piece + 1) * rows):
                for e in range(8):
                    at = (f, z, pl.ds(e * 8, 8))
                    first = image[at]
                    sol[at] = c * rhs[at] - d * first
                    res[at] = rhs[at] - c * first + d * twice[at]
            for k, (vmem, hbm) in enumerate(((sol, sol_hbm), (res, res_hbm))):
                copy = pltpu.make_async_copy(
                    vmem.at[f, part], hbm.at[f, part], sems.at[k, f, piece]
                )
                copy.start()
                copies.append(copy)
    for copy in copies:
        copy.wait()


def shards(source_terms, diffusion, mass_coefficient):
    shape = source_terms.shape
    field = (FIELDS, TILES, 8, LANES)
    f32 = jnp.float32
    operators = jnp.asarray(lane_operators())
    rhs, image, twice, coefs = pl.pallas_call(
        kernel,
        out_shape=tuple(
            jax.ShapeDtypeStruct(s, f32) for s in (shape, shape, shape, (2, 8, LANES))
        ),
        in_specs=[pl.BlockSpec(memory_space=pltpu.HBM)] * 4,
        out_specs=(pl.BlockSpec(memory_space=pltpu.VMEM),) * 4,
        scratch_shapes=[
            pltpu.VMEM(shape, f32),
            pltpu.VMEM(shape, f32),
            pltpu.VMEM(mass_coefficient.shape, f32),
            pltpu.VMEM((2, LANES, LANES), f32),
            pltpu.VMEM((2, 2 * LANES, 2 * LANES), jnp.bfloat16),
            pltpu.VMEM(field, f32),
            pltpu.VMEM(field[1:], f32),
            pltpu.VMEM((PHASES,) + field, f32),
            pltpu.VMEM((2,) + field, f32),
            pltpu.VMEM((2,) + field, f32),
            pltpu.VMEM((PHASES, FIELDS, 8, LANES), f32),
            pltpu.VMEM((PHASES, FIELDS, 2, 8, 8, LANES), f32),
            pltpu.VMEM((PHASES, FIELDS, 6, 8, LANES), f32),
            pltpu.VMEM((12, 8, LANES), f32),
            pltpu.VMEM((2, 1, LANES), f32),
            pltpu.VMEM((2, 15, 1, LANES), f32),
            pltpu.SemaphoreType.DMA((8,)),
            pltpu.SemaphoreType.DMA((PHASES, FIELDS, 8)),
            pltpu.SemaphoreType.DMA((PHASES, FIELDS, 8)),
            pltpu.SemaphoreType.DMA((2, 15)),
            pltpu.SemaphoreType.DMA((2, 15)),
        ],
        compiler_params=pltpu.CompilerParams(
            collective_id=0, has_side_effects=True, vmem_limit_bytes=40 * 1024 * 1024
        ),
    )(*(pltpu.with_memory_space_constraint(x, pltpu.HBM) for x in (source_terms, diffusion, mass_coefficient, operators)))
    return pl.pallas_call(
        combine,
        out_shape=(jax.ShapeDtypeStruct(shape, f32),) * 2,
        in_specs=[pl.BlockSpec(memory_space=pltpu.VMEM)] * 4,
        out_specs=(pl.BlockSpec(memory_space=pltpu.HBM),) * 2,
        scratch_shapes=[
            pltpu.VMEM(shape, f32),
            pltpu.VMEM(shape, f32),
            pltpu.SemaphoreType.DMA((2, FIELDS, PIECES)),
        ],
    )(*(pltpu.with_memory_space_constraint(x, pltpu.VMEM) for x in (rhs, image, twice, coefs)))


def solution(mesh):
    in_specs = (
        P(None, "axial", None, "azi"),
        P(None, "axial", None, "azi"),
        P("axial", None, "azi"),
    )
    out_specs = (P(None, "axial", None, "azi"), P(None, "axial", None, "azi"))
    return jax.shard_map(shards, mesh=mesh, in_specs=in_specs, out_specs=out_specs, check_vma=False)
```
